256 devices in a mesh: dp: 4 (over x), sample: 16 (over z, y_lo), tensor: 4 (over y_hi, core).
Axes of the slice: x: 4, y: 4 (y_hi: 2, y_lo: 2; y = y_hi * 2 + y_lo), z: 8, core: 2. Of those that a mesh axis runs over, the one named last changes fastest.
Arguments:
- prompt_x: bfloat16 [4, 2048, 8192], P('dp', 'sample', 'tensor'), may hold values from -6 to 6
- prompt_b: bfloat16 [4, 2048, 256], P('dp', 'sample'), may hold values from -0.06591797 to 0.06591797
- prompt_step: float32 [4, 128, 2048], P('dp', 'tensor', 'sample'), may hold values from 0.3 to 3
- resp_x: bfloat16 [4, 16, 512, 8192], P('dp', 'sample', None, 'tensor'), may hold values from -6 to 6
- resp_b: bfloat16 [4, 16, 512, 256], P('dp', 'sample'), may hold values from -0.06591797 to 0.06591797
- resp_c: bfloat16 [4, 16, 512, 256], P('dp', 'sample'), may hold values from -6 to 6
- resp_step: float32 [4, 16, 128, 512], P('dp', 'sample', 'tensor'), may hold values from 0.3 to 3
- decay_rate: float32 [128], P('tensor'), as said below
- skip_gain: float32 [128], P('tensor'), may hold values from 0.5 to 2
- lengths: int32 [4, 16], P('dp', 'sample'), may hold values from 1 to 512, 5120 in all within a row
- prompt_map: int32 [4], replicated, may hold values from 0 to 3
- resp_cotangent: bfloat16 [4, 16, 512, 8192], P('dp', 'sample', None, 'tensor'), may hold values from -6 to 6
Outputs:
- resp_y: bfloat16 [4, 16, 512, 8192], P('dp', 'sample', None, 'tensor')
- resp_dx: bfloat16 [4, 16, 512, 8192], P('dp', 'sample', None, 'tensor')
- prompt_dx: bfloat16 [4, 2048, 8192], P('dp', 'sample', 'tensor')
- skip_grad: float32 [128], P('tensor')
The draws below stay inside these ranges and needn't reach their ends.
Inputs may be any that keep to these rules, and one draw needn't show every extreme that they name: `lengths`: live tokens of each response; in each prompt group the counts sum to 5120, and one of them is exactly 512. `prompt_map`: the prompt of each group; several groups may continue the same prompt. `decay_rate`: positive rates.
All inputs are finite; a program needn't handle non-finite values.
Results may differ from the reference program's by a relative error of at most 0.0046.
Values sent between devices are 32-bit elements; how exact they have to be, the bound alone decides.
No kernel may reach another device: no remote copies, remote signals or barrier semaphores. Data moves between devices by JAX's collectives and lax.ppermute only.
A program may use at most 128 MiB of HBM per device.

```python
import math
import jax
import jax.numpy as jnp
import numpy as np
from jax import lax

HEADS = 128
HEAD_DIM = 64
STATE = 256
STRETCH = 256
RESP = 512
PROMPT_DEV = 128
PROMPT_LEN = 2048
N_DP = 4
N_SAMPLE = 16


def draw_decay_rate(key, part):
    key = jax.random.fold_in(key, 7)
    key_pick, key_slow, key_fast = jax.random.split(key, 3)
    slow_share = 0.5
    fast_top = 1.0 / 25.0
    span = float(PROMPT_LEN + RESP)
    slow_pick = jax.random.uniform(key_pick, (HEADS,), jnp.float32) < slow_share
    slow_rate = jnp.exp(jax.random.uniform(key_slow, (HEADS,), jnp.float32, math.log(0.1), math.log(0.8))) / span
    fast_rate = jnp.exp(jax.random.uniform(key_fast, (HEADS,), jnp.float32, math.log(1.0 / 190.0), math.log(fast_top)))
    return jnp.where(slow_pick, slow_rate, fast_rate).astype(jnp.float32)


def touch_ends(values, key, least, high):
    longest = values.shape.index(max(values.shape))
    spots = []
    for shift in (0, 1):
        where = [jax.random.randint(jax.random.fold_in(key, axis), (), 0, length) for axis, length in enumerate(values.shape)]
        where[longest] = (where[longest] + shift) % values.shape[longest]
        spots.append(tuple(where))
    return values.at[spots[0]].set(least).at[spots[1]].set(high)


def steps_of(own_key, shape, cuts, smallest, largest):
    def one(position, parts):
        draws = jax.random.uniform(jax.random.fold_in(jax.random.fold_in(own_key, 6), position), (parts,), jnp.float32, smallest / len(cuts), largest / len(cuts))
        return jnp.repeat(jnp.exp(draws), shape[position] // parts).reshape((-1,) + (1,) * (len(shape) - position - 1))

    level = one(*cuts[0])
    for cut in cuts[1:]:
        level = level * one(*cut)
    return level


def split_up(count, total, most, skew):
    loads = [(1 << 20) // math.isqrt(standing ** skew) + 1 for standing in range(2, count + 1)]
    surplus, given = total - most - (count - 1), [1] * (count - 1)
    while surplus > 0:
        candidates = [i for i in range(count - 1) if given[i] < most]
        pool, left = sum([loads[i] for i in candidates]), surplus
        for i in candidates:
            extra = min(most - given[i], max(1, left * loads[i] // pool), surplus)
            given[i] = given[i] + extra
            surplus = surplus - extra
    return np.array([most] + given)


def uneven_parts(own_key, amount, total, bound, skew):
    if amount == 2:
        one = jax.random.randint(own_key, (), max(1, total - bound), min(bound, total - 1) + 1)
        return jnp.stack([one, total - one])
    tallies = jnp.asarray(split_up(amount, total, bound, skew), jnp.int32)
    twos = (amount - 1) // 2
    donor, sink = tallies[1:1 + 2 * twos:2], tallies[2:2 + 2 * twos:2]
    slack = jnp.minimum(donor - 1, bound - sink)
    shifted = jax.random.randint(jax.random.fold_in(own_key, 1), (twos,), 0, 1 << 20) % (slack + 1)
    tallies = tallies.at[1:1 + 2 * twos:2].set(donor - shifted).at[2:2 + 2 * twos:2].set(sink + shifted)
    return tallies[jax.random.permutation(jax.random.fold_in(own_key, 2), amount)]


def gaussian(key, dims, width, bound, cuts=(), dtype=jnp.bfloat16):
    array = jax.random.normal(key, dims, jnp.float32) * width
    if len(cuts) > 0:
        array = steps_of(key, dims, cuts, -0.22, 0.18) * array
    return jnp.clip(array, min=-bound, max=bound).astype(dtype)


def setup_inputs(seed: int = 0) -> dict:
    splits = jax.random.split(jax.random.key(seed), 13)
    return {
        "prompt_x": gaussian(splits[0], (N_DP, PROMPT_LEN, HEADS * HEAD_DIM), 1.0, 6.0, ((0, 4), (1, 16), (2, 4))),
        "prompt_b": gaussian(splits[1], (N_DP, PROMPT_LEN, STATE), 0.011, 0.06591797, ((0, 4), (1, 16))),
        "prompt_step": jnp.clip(jnp.exp(math.log(3.0) - 2.3025851 * jax.random.uniform(splits[2], (N_DP, HEADS, PROMPT_LEN), jnp.float32) ** steps_of(splits[2], (N_DP, HEADS, PROMPT_LEN), ((0, 4), (1, 4), (2, 16)), -0.2, 0.2)), 0.3, 3.0),
        "resp_x": gaussian(splits[3], (N_DP, N_SAMPLE, RESP, HEADS * HEAD_DIM), 1.0, 6.0, ((0, 4), (1, 16), (3, 4))),
        "resp_b": gaussian(splits[4], (N_DP, N_SAMPLE, RESP, STATE), 0.011, 0.06591797, ((0, 4), (1, 16))),
        "resp_c": gaussian(splits[5], (N_DP, N_SAMPLE, RESP, STATE), 1.0, 6.0, ((0, 4), (1, 16))),
        "resp_step": jnp.clip(jnp.exp(math.log(3.0) - 2.3025851 * jax.random.uniform(splits[6], (N_DP, N_SAMPLE, HEADS, RESP), jnp.float32) ** steps_of(splits[6], (N_DP, N_SAMPLE, HEADS, RESP), ((0, 4), (1, 16), (2, 4)), -0.2, 0.2)), 0.3, 3.0),
        "decay_rate": draw_decay_rate(jax.random.fold_in(splits[12], 71), 0),
        "skip_gain": jnp.clip(0.5 + 1.5 * jax.random.uniform(splits[8], (HEADS,), jnp.float32) ** steps_of(splits[8], (HEADS,), ((0, 4),), -0.2, 0.2), 0.5, 2.0),
        "lengths": jax.vmap(lambda own: uneven_parts(own, N_SAMPLE, N_SAMPLE * RESP * 5 // 8, RESP, 2))(jax.random.split(splits[9], N_DP)).reshape((N_DP, N_SAMPLE)).astype(jnp.int32),
        "prompt_map": touch_ends(jax.random.randint(splits[10], (N_DP,), 0, N_DP), jax.random.fold_in(splits[10], 1), 0, N_DP - 1).astype(jnp.int32),
        "resp_cotangent": gaussian(splits[11], (N_DP, N_SAMPLE, RESP, HEADS * HEAD_DIM), 1.0, 6.0, ((0, 4), (1, 16), (3, 4))),
    }


def prompt_block(block_x, block_b, block_step, decay_rate):
    heads_count = block_step.shape[0]
    count = block_step.shape[1]
    log_step = -block_step * decay_rate[:, None]
    after_in = jnp.flip(jnp.cumsum(jnp.flip(log_step, 1), 1), 1) - log_step
    weight_coef = jnp.exp(after_in) * block_step
    weighted = (block_x.astype(jnp.float32).reshape(count, heads_count, HEAD_DIM) * weight_coef.T[:, :, None]).astype(jnp.bfloat16)
    contrib = jnp.einsum('thp,tn->hpn', weighted, block_b, preferred_element_type=jnp.float32)
    return (contrib, lax.optimization_barrier(jnp.sum(log_step, 1)), weight_coef)

def prompt_back(block_b, weight_coef, block_grad):
    count = block_b.shape[0]
    back = jnp.einsum('hpn,tn->thp', block_grad, block_b.astype(jnp.float32), precision=lax.Precision.HIGHEST)
    return (back * weight_coef.T[:, :, None]).reshape(count, -1).astype(jnp.bfloat16)

def response_pass(resp_float, start_state, skip_gain, resp_b, resp_c, step_size, decay_rate, length):
    tokens_count = resp_float.shape[0]
    heads_count = step_size.shape[0]
    blocks = tokens_count // STRETCH
    values = resp_float.reshape(blocks, STRETCH, heads_count, HEAD_DIM)
    key_raw = resp_b.reshape(blocks, STRETCH, STATE)
    query_raw = resp_c.reshape(blocks, STRETCH, STATE)
    key_rows = key_raw.astype(jnp.float32)
    query_rows = query_raw.astype(jnp.float32)
    log_step = (-step_size * decay_rate[:, None]).reshape(heads_count, blocks, STRETCH).transpose(1, 0, 2)
    step_blocks = step_size.reshape(heads_count, blocks, STRETCH).transpose(1, 0, 2)
    lower = jnp.tril(jnp.ones((STRETCH, STRETCH), bool))

    def advance(state, inputs):
        value_blk, key_blk, query_blk, key_half, query_half, log_blk, step_blk = inputs
        cumlog = jnp.cumsum(log_blk, axis=1)
        scores = jnp.dot(query_half, key_half.T, preferred_element_type=jnp.float32)
        log_gap = cumlog[:, :, None] - cumlog[:, None, :]
        decay_mat = jnp.exp(jnp.where(lower[None], log_gap, -jnp.inf))
        mixing = decay_mat * scores[None] * step_blk[:, None, :]
        inner = jnp.einsum('hij,jhp->ihp', mixing, value_blk, precision=lax.Precision.HIGHEST)
        carried = jnp.einsum('in,hpn->ihp', query_blk, state, precision=lax.Precision.HIGHEST) * jnp.exp(cumlog).T[:, :, None]
        tail = jnp.exp(cumlog[:, -1:] - cumlog) * step_blk
        new_state = jnp.exp(cumlog[:, -1])[:, None, None] * state + jnp.einsum('jhp,jn->hpn', value_blk * tail.T[:, :, None], key_blk, precision=lax.Precision.HIGHEST)
        return (new_state, inner + carried)
    final_state, outputs = lax.scan(advance, start_state, (values, key_rows, query_rows, key_raw, query_raw, log_step, step_blocks))
    outputs = outputs.reshape(tokens_count, heads_count, HEAD_DIM) + skip_gain[None, :, None] * resp_float.reshape(tokens_count, heads_count, HEAD_DIM)
    live = (jnp.arange(tokens_count) < length)[:, None, None]
    return jnp.where(live, outputs, 0.0).reshape(tokens_count, heads_count * HEAD_DIM)

def reference(prompt_x, prompt_b, prompt_step, resp_x, resp_b, resp_c, resp_step, decay_rate, skip_gain, lengths, prompt_map, resp_cotangent):
    states_list = []
    block_info = []
    for group in range(N_DP):
        block_xs = prompt_x[group].reshape(N_SAMPLE, PROMPT_DEV, HEADS * HEAD_DIM)
        block_bs = prompt_b[group].reshape(N_SAMPLE, PROMPT_DEV, STATE)
        block_steps = prompt_step[group].reshape(HEADS, N_SAMPLE, PROMPT_DEV).transpose(1, 0, 2)
        contrib, log_total, coefs = jax.vmap(prompt_block, in_axes=(0, 0, 0, None))(block_xs, block_bs, block_steps, decay_rate)
        after = jnp.flip(jnp.cumsum(jnp.flip(log_total, 0), 0), 0) - log_total
        states_list.append(lax.optimization_barrier(jnp.sum(jnp.exp(after)[:, :, None, None] * contrib, 0)))
        block_info.append((block_bs, coefs, after))
    prompt_states = jnp.stack(states_list)
    outs_y = []
    outs_dx = []
    group_grads = []
    skip_total = jnp.zeros((HEADS,), jnp.float32)
    for group in range(N_DP):
        start_state = prompt_states[prompt_map[group]]

        def one_response(inputs):
            x_rows, b_rows, c_rows, step_rows, length, cot_rows = inputs

            def forward(resp_float, first_state, gains):
                return response_pass(resp_float, first_state, gains, b_rows, c_rows, step_rows, decay_rate, length)
            result, pullback = jax.vjp(forward, x_rows.astype(jnp.float32), start_state, skip_gain)
            grad_x, grad_state, grad_gain = pullback(cot_rows.astype(jnp.float32))
            return (result.astype(jnp.bfloat16), grad_x.astype(jnp.bfloat16), grad_state, grad_gain)
        ys, dxs, dstates, dgains = lax.map(one_response, (resp_x[group], resp_b[group], resp_c[group], resp_step[group], lengths[group], resp_cotangent[group]))
        outs_y.append(ys)
        outs_dx.append(dxs)
        group_grads.append(lax.optimization_barrier(jnp.sum(dstates, 0)))
        skip_total = skip_total + lax.optimization_barrier(jnp.sum(dgains, 0))
    group_grads = jnp.stack(group_grads)
    prompt_out = []
    for prompt in range(N_DP):
        pick = (prompt_map == prompt).astype(jnp.float32)
        prompt_grad = lax.optimization_barrier(jnp.sum(pick[:, None, None, None] * group_grads, 0))
        block_bs, coefs, after = block_info[prompt]
        block_grads = jnp.exp(after)[:, :, None, None] * prompt_grad[None]
        pieces = jax.vmap(prompt_back)(block_bs, coefs, block_grads)
        prompt_out.append(pieces.reshape(PROMPT_LEN, HEADS * HEAD_DIM))
    return (jnp.stack(outs_y), jnp.stack(outs_dx), jnp.stack(prompt_out), skip_total)
```

```python
import functools

import jax
import jax.numpy as jnp
from jax import lax
from jax.experimental import pallas as pl
from jax.experimental.pallas import tpu as pltpu
from jax.sharding import PartitionSpec as P

F32 = jnp.float32
BF16 = jnp.bfloat16
LOG2E = 1.4426950408889634
EXACT = lax.Precision.HIGHEST
TILE = 128
HALF = 64
RING = 8
VMEM = pl.BlockSpec(memory_space=pltpu.VMEM)
SMEM = pl.BlockSpec(memory_space=pltpu.SMEM)


def dot(left, right, dims=((1,), (0,)), precision=None):
    return lax.dot_general(
        left, right, (dims, ((), ())), precision=precision, preferred_element_type=F32
    )


def iota(shape, axis):
    return lax.broadcasted_iota(jnp.int32, shape, axis)


def params(megabytes=40):
    return pltpu.CompilerParams(vmem_limit_bytes=megabytes << 20)


def spread(cols, first, low):
    return jnp.where(low, cols[:, first : first + 1], cols[:, first + 1 : first + 2])


def weigh_kernel(pos, x_ref, b_ref, step_ref, rate_ref, send_ref, own_ref, cols_ref):
    even = pos[1] == 0
    step = step_ref[...]
    heads = step.shape[0]
    log = -(step * rate_ref[...])
    square = (TILE, TILE)
    later = (iota(square, 0) > iota(square, 1)).astype(F32)
    coef = jnp.exp(dot(log, later, precision=EXACT)) * step
    total = jnp.broadcast_to(jnp.sum(log, 1, keepdims=True), (heads, TILE))
    blank = jnp.zeros((TILE - 2 * heads, TILE), F32)
    cols = jnp.concatenate([coef, total, blank], 0).T
    cols_ref[...] = cols
    low = iota(square, 1) < HALF
    for place in range(RING):
        pair = []
        for part in range(2):
            tile = 2 * place + part
            x = x_ref[:, tile * TILE : (tile + 1) * TILE].astype(F32)
            pair.append(x * spread(cols, 2 * tile, low))
        own_ref[place] = jnp.where(even, pair[0], pair[1]).astype(BF16)
        send_ref[place] = jnp.where(even, pair[1], pair[0]).astype(BF16).astype(F32)
    send_ref[RING] = b_ref[:, :TILE].astype(F32)
    send_ref[RING + 1] = b_ref[:, TILE:].astype(F32)


def weigh(pos, x, b, step, rate):
    return pl.pallas_call(
        weigh_kernel,
        out_shape=(
            jax.ShapeDtypeStruct((RING + 2, TILE, TILE), F32),
            jax.ShapeDtypeStruct((RING, TILE, TILE), BF16),
            jax.ShapeDtypeStruct((TILE, TILE), F32),
        ),
        in_specs=[SMEM, VMEM, VMEM, VMEM, VMEM],
        out_specs=(VMEM, VMEM, VMEM),
        compiler_params=params(),
        cost_estimate=pl.CostEstimate(flops=10**6, bytes_accessed=4 << 20, transcendentals=0),
        name="weigh",
    )(pos, x, b, step, rate)


def start_grad_kernel(
    pos, dy_ref, x_ref, c_ref, step_ref, rate_ref,
    send_ref, keep_ref, pair_ref, cols_ref, rows_ref, turned,
):
    group = pl.program_id(0)
    even = pos[1] == 0
    length = pos[2]
    tokens = dy_ref.shape[0]
    blocks = tokens // TILE
    square = (TILE, TILE)

    @pl.when(group == 0)
    def _():
        step = step_ref[...]
        heads = step.shape[0]
        log = step * rate_ref[...] * (-LOG2E)
        upto = (iota(square, 0) <= iota(square, 1)).astype(F32)
        run = jnp.zeros((heads, 1), F32)
        for block in range(blocks):
            at = slice(block * TILE, (block + 1) * TILE)
            turned[:, at] = c_ref[at, :].astype(F32).T.astype(BF16)
            cum = dot(log[:, at], upto, precision=EXACT)
            rows_ref[:, at] = cum
            whole = cum + run
            run = whole[:, TILE - 1 :]
            live = iota((heads, TILE), 1) + block * TILE < length
            entry = jnp.where(live, jnp.exp2(whole), 0.0)
            blank = jnp.zeros((TILE - 3 * heads, TILE), F32)
            cols_ref[at, :] = jnp.concatenate([cum, step[:, at], entry, blank], 0).T

    low = iota(square, 1) < HALF
    shift = lax.rem(TILE - 4 * group, TILE)
    weighted = []
    gains = [jnp.zeros((1, TILE), F32)] * 2
    for block in range(blocks):
        at = slice(block * TILE, (block + 1) * TILE)
        cols = pltpu.roll(cols_ref[at, :], shift, 1)
        live = iota(square, 0) + block * TILE < length
        row = []
        for part in range(2):
            lanes = slice(part * TILE, (part + 1) * TILE)
            dy = dy_ref[at, lanes].astype(F32)
            row.append((dy * spread(cols, 64 + 2 * part, low)).astype(BF16))
            product = jnp.where(live, dy * x_ref[at, lanes].astype(F32), 0.0)
            gains[part] = gains[part] + jnp.sum(product, 0, keepdims=True)
        weighted.append(jnp.concatenate(row, 1))
    grad = dot(turned[...], jnp.concatenate(weighted, 0))
    first, second = grad[:, :TILE], grad[:, TILE:]
    keep_ref[0] = jnp.where(even, first[:TILE], second[:TILE])
    send_ref[0] = jnp.where(even, second[:TILE], first[:TILE])
    for part, value in enumerate((first, second)):
        pair_ref[0, part, :TILE] = value[TILE:]
        pair_ref[0, part, TILE:] = jnp.broadcast_to(gains[part], (8, TILE))


def start_grad(pos, dy, x, c, step, rate):
    tokens, width = dy.shape
    state = c.shape[1]
    heads = step.shape[0]
    group = width // RING
    turn = lambda i, pos: (lax.rem(i - pos[0] + RING, RING), 0, 0)
    whole = lambda shape: pl.BlockSpec(shape, lambda i, pos: (0, 0))
    return pl.pallas_call(
        start_grad_kernel,
        grid_spec=pltpu.PrefetchScalarGridSpec(
            num_scalar_prefetch=1,
            grid=(RING,),
            in_specs=[
                pl.BlockSpec((tokens, group), lambda i, pos: (0, i)),
                pl.BlockSpec((tokens, group), lambda i, pos: (0, i)),
                whole((tokens, state)),
                whole((heads, tokens)),
                whole((heads, 1)),
            ],
            out_specs=(
                pl.BlockSpec((1, TILE, TILE), turn),
                pl.BlockSpec((1, TILE, TILE), turn),
                pl.BlockSpec((1, 2, TILE + 8, TILE), lambda i, pos: turn(i, pos) + (0,)),
                whole((tokens, TILE)),
                whole((heads, tokens)),
            ),
            scratch_shapes=[pltpu.VMEM((state, tokens), BF16)],
        ),
        out_shape=(
            jax.ShapeDtypeStruct((RING, TILE, TILE), F32),
            jax.ShapeDtypeStruct((RING, TILE, TILE), F32),
            jax.ShapeDtypeStruct((RING, 2, TILE + 8, TILE), F32),
            jax.ShapeDtypeStruct((tokens, TILE), F32),
            jax.ShapeDtypeStruct((heads, tokens), F32),
        ),
        compiler_params=params(),
        cost_estimate=pl.CostEstimate(
            flops=2 * tokens * width * state, bytes_accessed=16 << 20, transcendentals=0
        ),
        name="start_grad",
    )(pos, dy, x, c, step, rate)


def contrib_kernel(pos, own_ref, got_ref, b_ref, fade_ref, fade_got_ref, out_ref, turned):
    place = pl.program_id(0)

    @pl.when(place == 0)
    def _():
        for part in range(2):
            at = slice(part * TILE, (part + 1) * TILE)
            turned[0, at] = b_ref[:, at].astype(F32).T.astype(BF16)
            turned[1, at] = got_ref[RING + part].T.astype(BF16)

    low = iota((8, TILE), 1) < HALF
    shift = lax.rem(2 * TILE - 32 - 4 * place - 2 * pos[1], TILE)
    scale = spread(pltpu.roll(fade_ref[...], shift, 1), 0, low)[:1]
    scale_got = spread(pltpu.roll(fade_got_ref[...], shift, 1), 0, low)[:1]
    own = dot(turned[0], own_ref[0])
    got = dot(turned[1], got_ref[place].astype(BF16))
    out_ref[0] = own * scale + got * scale_got


def contributions(pos, own, got, b, fade, fade_got):
    state = b.shape[1]
    whole = lambda shape: pl.BlockSpec(shape, lambda i, pos: (0,) * len(shape))
    return pl.pallas_call(
        contrib_kernel,
        grid_spec=pltpu.PrefetchScalarGridSpec(
            num_scalar_prefetch=1,
            grid=(RING,),
            in_specs=[
                pl.BlockSpec((1, TILE, TILE), lambda i, pos: (i, 0, 0)),
                whole(got.shape),
                whole(b.shape),
                whole(fade.shape),
                whole(fade.shape),
            ],
            out_specs=pl.BlockSpec(
                (1, state, TILE), lambda i, pos: (lax.rem(i - pos[0] + RING, RING), 0, 0)
            ),
            scratch_shapes=[pltpu.VMEM((2, state, TILE), BF16)],
        ),
        out_shape=jax.ShapeDtypeStruct((RING, state, TILE), F32),
        compiler_params=params(),
        cost_estimate=pl.CostEstimate(flops=10**8, bytes_accessed=4 << 20, transcendentals=0),
        name="contributions",
    )(pos, own, got, b, fade, fade_got)


def mix_kernel(
    base, pos, x_ref, dy_ref, b_ref, c_ref, cols_ref, rows_ref, gain_ref, *rest
):
    y_ref, dx_ref, scores, scores_t, b_turned, c_turned, inner_dx, out_scale, wdy = rest[-9:]
    step_index = pl.program_id(0)
    group = step_index + base
    length = pos[2]
    tokens = x_ref.shape[0]
    blocks = tokens // TILE
    square = (TILE, TILE)

    @pl.when(step_index == 0)
    def _():
        upper = iota(square, 0) <= iota(square, 1)
        lower = iota(square, 0) >= iota(square, 1)
        for block in range(blocks):
            at = slice(block * TILE, (block + 1) * TILE)
            b_rows, c_rows = b_ref[at, :], c_ref[at, :]
            scores[block] = jnp.where(lower, dot(c_rows, b_rows, ((1,), (1,))), 0.0)
            scores_t[block] = jnp.where(upper, dot(b_rows, c_rows, ((1,), (1,))), 0.0)
            b_turned[:, at] = b_rows.astype(F32).T.astype(BF16)
            c_turned[:, at] = c_rows.astype(F32).T.astype(BF16)

    low = iota(square, 1) < HALF
    shift = lax.rem(TILE - 4 * group, TILE)

    def split(value):
        return jnp.concatenate(
            [jnp.where(low, value, 0.0), jnp.where(low, 0.0, value)], 0
        ).astype(BF16)

    state = None
    ends = []
    for block in range(blocks):
        at = slice(block * TILE, (block + 1) * TILE)
        cols = pltpu.roll(cols_ref[at, :], shift, 1)
        live = iota(square, 0) + block * TILE < length
        eight = rows_ref[pl.ds(pl.multiple_of(group // 2 * 8, 8), 8), at]
        rows = jnp.where(group % 2 == 0, eight[:4], eight[4:])
        update, end = [], []
        if state is not None:
            carried = dot(c_ref[at, :], state.astype(BF16))
        for part in range(2):
            lanes = slice(part * TILE, (part + 1) * TILE)
            x = x_ref[at, lanes].astype(F32)
            dy = jnp.where(live, dy_ref[at, lanes].astype(F32), 0.0)
            gain = gain_ref[:, lanes]
            sides = [
                jnp.broadcast_to(cols[:, 2 * part + k : 2 * part + k + 1], square)
                for k in range(2)
            ]
            step = spread(cols, 32 + 2 * part, low)
            log = jnp.where(low, sides[0], sides[1])
            last = log[TILE - 1 :]
            since = jnp.exp2(log)
            until = jnp.exp2(last - log)
            ahead, back = [], []
            for k in range(2):
                gap = sides[k] - rows[2 * part + k : 2 * part + k + 1]
                ahead.append((jnp.exp2(jnp.minimum(gap, 0.0)) * scores[block]).astype(BF16))
                back.append((jnp.exp2(jnp.minimum(-gap, 0.0)) * scores_t[block]).astype(BF16))
            stepped = x * step
            y = dot(jnp.concatenate(ahead, 1), split(stepped)) + gain * x
            if state is not None:
                y = y + since * carried[:, lanes]
            y_ref[at, lanes] = jnp.where(live, y, 0.0)
            dx = dot(jnp.concatenate(back, 1), split(dy))
            inner_dx[at, lanes] = step * dx + gain * dy
            out_scale[at, lanes] = step * until
            wdy[at, lanes] = (dy * since).astype(BF16)
            update.append((stepped * until).astype(BF16))
            end.append(jnp.exp2(last))
        ends.append(jnp.concatenate(end, 1))
        if block < blocks - 1:
            grown = dot(b_turned[:, at], jnp.concatenate(update, 1))
            state = grown if state is None else ends[block] * state + grown

    grad = None
    for block in reversed(range(blocks)):
        at = slice(block * TILE, (block + 1) * TILE)
        dx = inner_dx[at, :]
        if grad is not None:
            dx = dx + out_scale[at, :] * dot(b_ref[at, :], grad.astype(BF16))
        dx_ref[at, :] = dx.astype(BF16)
        if block > 0:
            grown = dot(c_turned[:, at], wdy[at, :])
            grad = grown if grad is None else ends[block] * grad + grown


def mix(base, count, pos, x, dy, b, c, cols, rows, gain, before):
    tokens, width = x.shape
    state = b.shape[1]
    group = width // RING
    own = pl.BlockSpec((tokens, group), lambda i, pos: (0, i + base))
    whole = lambda shape: pl.BlockSpec(shape, lambda i, pos: (0, 0))
    specs = [
        own, own, whole(b.shape), whole(c.shape), whole(cols.shape), whole(rows.shape),
        pl.BlockSpec((1, group), lambda i, pos: (0, i + base)),
    ]
    operands = [x, dy, b, c, cols, rows, gain]
    alias = {}
    if before is not None:
        specs += [pl.BlockSpec(memory_space=pl.ANY)] * 2
        operands += list(before)
        alias = {8: 0, 9: 1}
    blocks = tokens // TILE
    return pl.pallas_call(
        functools.partial(mix_kernel, base),
        grid_spec=pltpu.PrefetchScalarGridSpec(
            num_scalar_prefetch=1,
            grid=(count,),
            in_specs=specs,
            out_specs=(own, own),
            scratch_shapes=[
                pltpu.VMEM((blocks, TILE, TILE), F32),
                pltpu.VMEM((blocks, TILE, TILE), F32),
                pltpu.VMEM((state, tokens), BF16),
                pltpu.VMEM((state, tokens), BF16),
                pltpu.VMEM((tokens, group), F32),
                pltpu.VMEM((tokens, group), F32),
                pltpu.VMEM((tokens, group), BF16),
            ],
        ),
        out_shape=(
            jax.ShapeDtypeStruct((tokens, width), F32),
            jax.ShapeDtypeStruct((tokens, width), BF16),
        ),
        input_output_aliases=alias,
        compiler_params=params(),
        cost_estimate=pl.CostEstimate(
            flops=count * 8 * tokens * group * state,
            bytes_accessed=count * (4 << 20),
            transcendentals=0,
        ),
        name="mix",
    )(pos, *operands)


def finish_kernel(pos, c_ref, cols_ref, y_ref, own_ref, got_ref, pair_ref, out_ref):
    group = lax.rem(pl.program_id(0) + pos[0], RING)
    even = pos[1] == 0
    tokens = y_ref.shape[0]
    own, got = own_ref[0], got_ref[0]
    top = jnp.concatenate([jnp.where(even, own, got), jnp.where(even, got, own)], 1)
    bottom = jnp.concatenate([pair_ref[0, 0], pair_ref[0, 1]], 1)
    state = jnp.concatenate([top, bottom], 0).astype(BF16)
    low = iota((TILE, TILE), 1) < HALF
    shift = lax.rem(TILE - 4 * group, TILE)
    for block in range(tokens // TILE):
        at = slice(block * TILE, (block + 1) * TILE)
        cols = pltpu.roll(cols_ref[at, :], shift, 1)
        carried = dot(c_ref[at, :], state)
        for part in range(2):
            lanes = slice(part * TILE, (part + 1) * TILE)
            y = y_ref[at, lanes] + spread(cols, 64 + 2 * part, low) * carried[:, lanes]
            out_ref[at, lanes] = y.astype(BF16)


def finish(pos, c, cols, y, own, got, pair):
    tokens, width = y.shape
    group = width // RING
    whole = lambda shape: pl.BlockSpec(shape, lambda i, pos: (0, 0))
    turned = pl.BlockSpec((tokens, group), lambda i, pos: (0, lax.rem(i + pos[0], RING)))
    return pl.pallas_call(
        finish_kernel,
        grid_spec=pltpu.PrefetchScalarGridSpec(
            num_scalar_prefetch=1,
            grid=(RING,),
            in_specs=[
                whole(c.shape),
                whole(cols.shape),
                turned,
                pl.BlockSpec((1, TILE, TILE), lambda i, pos: (i, 0, 0)),
                pl.BlockSpec((1, TILE, TILE), lambda i, pos: (i, 0, 0)),
                pl.BlockSpec((1, 2, TILE, TILE), lambda i, pos: (i, 0, 0, 0)),
            ],
            out_specs=turned,
        ),
        out_shape=jax.ShapeDtypeStruct((tokens, width), BF16),
        compiler_params=params(),
        cost_estimate=pl.CostEstimate(
            flops=2 * tokens * width * 256, bytes_accessed=10 << 20, transcendentals=0
        ),
        name="finish",
    )(pos, c, cols, y, own, got, pair)


def back_kernel(b_ref, got_ref, *rest):
    grads, (own_ref, send_ref, gains_ref) = rest[:RING], rest[RING:]
    mine = b_ref[...]
    other = jnp.concatenate([got_ref[RING], got_ref[RING + 1]], 1).astype(BF16)
    state = mine.shape[1]
    for place in range(RING):
        grad = grads[place][:state].astype(BF16)
        own_ref[place] = dot(mine, grad)
        send_ref[place, :TILE] = dot(other, grad)
        send_ref[place, TILE:] = grads[place][state:]
        gains_ref[place] = grads[place][state:]


def back(b, got, grads):
    return pl.pallas_call(
        back_kernel,
        out_shape=(
            jax.ShapeDtypeStruct((RING, TILE, TILE), F32),
            jax.ShapeDtypeStruct((RING, TILE + 8, TILE), F32),
            jax.ShapeDtypeStruct((RING, 8, TILE), F32),
        ),
        in_specs=[VMEM] * (2 + RING),
        out_specs=(VMEM, VMEM, VMEM),
        compiler_params=params(),
        cost_estimate=pl.CostEstimate(flops=10**8, bytes_accessed=4 << 20, transcendentals=0),
        name="back",
    )(b, got, *grads)


def prompt_dx_kernel(pos, own_ref, gains_ref, got_ref, cols_ref, fade_ref, out_ref, skip_ref):
    group = lax.rem(pl.program_id(0) + pos[0], RING)
    even = pos[1] == 0
    low = iota((TILE, TILE), 1) < HALF
    cols = cols_ref[...] * fade_ref[0:1, :]
    cols = pltpu.roll(cols, lax.rem(TILE - 4 * group, TILE), 1)
    own, got = own_ref[0], got_ref[0, :TILE]
    tiles = (jnp.where(even, own, got), jnp.where(even, got, own))
    for part in range(2):
        lanes = slice(part * TILE, (part + 1) * TILE)
        out_ref[:, lanes] = (tiles[part] * spread(cols, 2 * part, low)).astype(BF16)
    own, got = gains_ref[0], got_ref[0, TILE:]
    skip_ref[0, 0] = jnp.where(even, own, got)
    skip_ref[0, 1] = jnp.where(even, got, own)


def prompt_gradient(pos, own, gains, got, cols, fade):
    block = lambda i, pos: (i, 0, 0)
    whole = lambda shape: pl.BlockSpec(shape, lambda i, pos: (0, 0))
    turn = lambda i, pos: lax.rem(i + pos[0], RING)
    return pl.pallas_call(
        prompt_dx_kernel,
        grid_spec=pltpu.PrefetchScalarGridSpec(
            num_scalar_prefetch=1,
            grid=(RING,),
            in_specs=[
                pl.BlockSpec((1, TILE, TILE), block),
                pl.BlockSpec((1, 8, TILE), block),
                pl.BlockSpec((1, TILE + 8, TILE), block),
                whole(cols.shape),
                whole(fade.shape),
            ],
            out_specs=(
                pl.BlockSpec((TILE, 2 * TILE), lambda i, pos: (0, turn(i, pos))),
                pl.BlockSpec((1, 2, 8, TILE), lambda i, pos: (turn(i, pos), 0, 0, 0)),
            ),
        ),
        out_shape=(
            jax.ShapeDtypeStruct((TILE, RING * 2 * TILE), BF16),
            jax.ShapeDtypeStruct((RING, 2, 8, TILE), F32),
        ),
        compiler_params=params(),
        cost_estimate=pl.CostEstimate(flops=10**6, bytes_accessed=2 << 20, transcendentals=0),
        name="prompt_gradient",
    )(pos, own, gains, got, cols, fade)


def along_z(value, distance):
    pairs = [
        (2 * z + y, 2 * ((z + distance) % RING) + y) for z in range(RING) for y in range(2)
    ]
    return lax.ppermute(value, "sample", pairs)


def swap(value, bit):
    return lax.ppermute(value, "sample", [(s, s ^ bit) for s in range(2 * RING)])


def along_dp(value, distance):
    return lax.ppermute(value, "dp", [(i, (i + distance) % 4) for i in range(4)])


def sum_at_owner(piece):
    down = along_z(jnp.stack([piece(6), piece(4)]), -1)
    up = along_z(piece(2), 1)
    far_up = along_z(piece(3), 3)
    near = along_z(piece(7) + down[0], -1)
    far = along_z(piece(5) + down[1], -3)
    above = along_z(piece(1) + up, 1)
    return piece(0) + far_up + near + far + above


def from_all(own):
    one, seven = along_z(own, -1), along_z(own, 1)
    three, five = along_z(own, -3), along_z(own, 3)
    two_four = along_z(jnp.stack([one, three]), -1)
    six = along_z(seven, 1)
    return [own, one, two_four[0], three, two_four[1], five, six, seven]


def body(
    prompt_x, prompt_b, prompt_step, resp_x, resp_b, resp_c, resp_step,
    decay_rate, skip_gain, lengths, prompt_map, resp_cotangent,
):
    place = lax.axis_index("sample")
    here = lax.axis_index("dp")
    parity = place % 2
    pos = jnp.stack([place // 2, parity, lengths[0, 0]]).astype(jnp.int32)
    rate = decay_rate[:, None]
    gain = jnp.repeat(skip_gain, HALF)[None]
    x, dy, b, c = resp_x[0, 0], resp_cotangent[0, 0], resp_b[0, 0], resp_c[0, 0]
    state = b.shape[1]

    send, own, coef = weigh(pos, prompt_x[0], prompt_b[0], prompt_step[0], rate)
    got = swap(send, 1)
    total = coef[:8]
    other = swap(total, 1)
    after_own = jnp.where(parity == 0, other, 0.0)
    after_got = jnp.where(parity == 0, 0.0, total)
    total = total + other
    for bit in (2, 4, 8):
        other = swap(total, bit)
        later = jnp.where(place & bit == 0, other, 0.0)
        after_own, after_got, total = after_own + later, after_got + later, total + other

    sent, kept, pair, cols, rows = start_grad(pos, dy, x, c, resp_step[0, 0], rate)
    came = swap(sent, 1)
    low_pair = sum_at_owner(lambda r: pair[r])
    low_own = jnp.where(parity == 0, low_pair[0], low_pair[1])
    low_other = jnp.where(parity == 0, low_pair[1], low_pair[0])
    high = sum_at_owner(lambda r: kept[r] + came[r])
    low = low_own + swap(low_other, 1)
    share = jnp.concatenate([high, low], 0)

    fade, fade_got = jnp.exp(after_own), jnp.exp(after_got)
    parts = contributions(pos, own, got, prompt_b[0], fade, fade_got)
    final = sum_at_owner(lambda r: parts[r])

    shares = [share] + [along_dp(share, d) for d in (1, 2, 3)]
    gradient, gains = 0.0, 0.0
    for distance, part in enumerate(shares):
        chosen = prompt_map[(here - distance) % 4] == here
        gradient = gradient + jnp.where(chosen, part[:state], 0.0)
        gains = gains + part[state:]
    share = jnp.concatenate([gradient, gains], 0)

    finals = [final] + [along_dp(final, d) for d in (1, 2, 3)]
    distance = (here - prompt_map[here]) % 4
    start = finals[0]
    for d in (1, 2, 3):
        start = jnp.where(distance == d, finals[d], start)

    mixed = None
    calls = 4
    for call in range(calls):
        count = RING // calls
        mixed = mix(call * count, count, pos, x, dy, b, c, cols, rows, gain, mixed)

    own_dx, send_dx, own_gains = back(prompt_b[0], got, from_all(share))
    got_dx = swap(send_dx, 1)

    high, low = start[:TILE], start[TILE:]
    highs = jnp.stack(from_all(high))
    highs_got = swap(highs, 1)
    low_got = swap(low, 1)
    low_pair = jnp.stack(
        [jnp.where(parity == 0, low, low_got), jnp.where(parity == 0, low_got, low)]
    )
    lows = jnp.stack(from_all(low_pair))
    resp_y = finish(pos, c, cols, mixed[0], highs, highs_got, lows)

    fade_row = jnp.roll(fade, -32, 1)
    prompt_dx, skip = prompt_gradient(pos, own_dx, own_gains, got_dx, coef, fade_row)
    skip_grad = jnp.sum(skip[:, :, 0].reshape(-1, HALF), 1)
    return (resp_y[None, None], mixed[1][None, None], prompt_dx[None], skip_grad)


def solution(mesh):
    placed = (
        P("dp", "sample", "tensor"),
        P("dp", "sample", None),
        P("dp", "tensor", "sample"),
        P("dp", "sample", None, "tensor"),
        P("dp", "sample", None, None),
        P("dp", "sample", None, None),
        P("dp", "sample", "tensor", None),
        P("tensor"),
        P("tensor"),
        P("dp", "sample"),
        P(),
        P("dp", "sample", None, "tensor"),
    )
    return jax.shard_map(
        body,
        mesh=mesh,
        in_specs=placed,
        out_specs=(
            P("dp", "sample", None, "tensor"),
            P("dp", "sample", None, "tensor"),
            P("dp", "sample", "tensor"),
            P("tensor"),
        ),
        check_vma=False,
    )
```

```python
import functools

import jax
import jax.numpy as jnp
from jax import lax
from jax.experimental import pallas as pl
from jax.experimental.pallas import tpu as pltpu
from jax.sharding import PartitionSpec as P

F32 = jnp.float32
BF16 = jnp.bfloat16
LOG2E = 1.4426950408889634
EXACT = lax.Precision.HIGHEST
TILE = 128
HALF = 64
RING = 8
PAIR = 2 * TILE
FULL = 3 * TILE + 8
UPPER = 112
MESSAGE = UPPER + 2 * TILE + 8
KEPT = (0, 1, 5, 7)
VMEM = pl.BlockSpec(memory_space=pltpu.VMEM)
SMEM = pl.BlockSpec(memory_space=pltpu.SMEM)
HBM = pl.BlockSpec(memory_space=pltpu.HBM)


def dot(left, right, dims=((1,), (0,)), precision=None):
    return lax.dot_general(
        left, right, (dims, ((), ())), precision=precision, preferred_element_type=F32
    )


def iota(shape, axis):
    return lax.broadcasted_iota(jnp.int32, shape, axis)


def along(pos):
    return pos[0] >> 1


def is_even(pos):
    return pos[0] & 1 == 0


def column(row):
    heads = row.shape[1]
    square = (heads, heads)
    return jnp.sum(jnp.where(iota(square, 0) == iota(square, 1), row, 0.0), 1, keepdims=True)


def params(megabytes=24):
    return pltpu.CompilerParams(vmem_limit_bytes=megabytes << 20)


def spread(cols, first, low):
    return jnp.where(low, cols[:, first : first + 1], cols[:, first + 1 : first + 2])


def weigh_kernel(pos, x_ref, b_ref, step_ref, rate_ref, send_ref, own_ref, cols_ref):
    even = is_even(pos)
    step = step_ref[...]
    heads = step.shape[0]
    log = -(step * column(rate_ref[...]))
    square = (TILE, TILE)
    later = (iota(square, 0) > iota(square, 1)).astype(F32)
    coef = jnp.exp(dot(log, later, precision=EXACT)) * step
    total = jnp.broadcast_to(jnp.sum(log, 1, keepdims=True), (heads, TILE))
    blank = jnp.zeros((TILE - 2 * heads, TILE), F32)
    cols = jnp.concatenate([coef, total, blank], 0).T
    cols_ref[...] = cols
    low = iota(square, 1) < HALF
    for place in range(RING):
        pair = []
        for part in range(2):
            tile = 2 * place + part
            x = x_ref[:, tile * TILE : (tile + 1) * TILE].astype(F32)
            pair.append(x * spread(cols, 2 * tile, low))
        own_ref[place] = jnp.where(even, pair[0], pair[1]).astype(BF16)
        send_ref[place] = jnp.where(even, pair[1], pair[0]).astype(BF16).astype(F32)
    send_ref[RING] = b_ref[:, :TILE].astype(F32)
    send_ref[RING + 1] = b_ref[:, TILE:].astype(F32)


def weigh(pos, x, b, step, rate):
    return pl.pallas_call(
        weigh_kernel,
        out_shape=(
            jax.ShapeDtypeStruct((RING + 2, TILE, TILE), F32),
            jax.ShapeDtypeStruct((RING, TILE, TILE), BF16),
            jax.ShapeDtypeStruct((TILE, TILE), F32),
        ),
        in_specs=[SMEM, VMEM, VMEM, VMEM, VMEM],
        out_specs=(VMEM, VMEM, VMEM),
        compiler_params=params(),
        cost_estimate=pl.CostEstimate(flops=10**6, bytes_accessed=4 << 20, transcendentals=0),
        name="weigh",
    )(pos, x, b, step, rate)


def sum_logs_kernel(step_ref, rate_ref, out_ref):
    log = -(step_ref[...] * column(rate_ref[...]))
    heads = log.shape[0]
    total = dot(jnp.ones((8, TILE), F32), log, ((1,), (1,)), EXACT)
    blank = jnp.zeros((8, TILE - 2 * heads), F32)
    out_ref[...] = jnp.concatenate([jnp.zeros((8, heads), F32), total, blank], 1)


def sum_logs(step, rate):
    return pl.pallas_call(
        sum_logs_kernel,
        out_shape=jax.ShapeDtypeStruct((8, TILE), F32),
        in_specs=[VMEM, VMEM],
        out_specs=VMEM,
        compiler_params=params(61),
        cost_estimate=pl.CostEstimate(flops=10**5, bytes_accessed=1 << 15, transcendentals=0),
        name="sum_logs",
    )(step, rate)


def scale_of(group, entries_ref, width):
    head = 4 * group + iota((TILE, width), 1) // HALF
    row = iota((TILE, width), 0)
    chosen = (row < 64) & (row % 32 == head)
    return dot(entries_ref[...], chosen.astype(F32).astype(BF16))


def weigh_group(group, dy_ref, entries_ref, weighted):
    width = weighted.shape[1]
    at = pl.ds(pl.multiple_of(group * width, width), width)
    scale = scale_of(group, entries_ref, width)
    weighted[...] = (dy_ref[:, at].astype(F32) * scale).astype(BF16)


def first_grads_kernel(
    pos, dy_ref, c_ref, step_ref, rate_ref, gain_ref,
    down_ref, up_ref, cols_ref, rows_ref, turned, entries_ref, weighted,
):
    length = pos[2]
    tokens = dy_ref.shape[0]
    square = (TILE, TILE)
    step = step_ref[...]
    heads = step.shape[0]
    log = step * column(rate_ref[...]) * (-LOG2E)
    gain = jnp.broadcast_to(column(gain_ref[...]), (heads, TILE))
    upto = (iota(square, 0) <= iota(square, 1)).astype(F32)
    run = jnp.zeros((heads, 1), F32)
    blank = jnp.zeros((TILE - 2 * heads, TILE), F32)
    for block in range(tokens // TILE):
        at = slice(block * TILE, (block + 1) * TILE)
        turned[:, at] = c_ref[at, :].astype(F32).T.astype(BF16)
        cum = dot(log[:, at], upto, precision=EXACT)
        rows_ref[:, at] = cum
        whole = cum + run
        run = whole[:, TILE - 1 :]
        live = iota((heads, TILE), 1) + block * TILE < length
        entry = jnp.where(live, jnp.exp2(whole), 0.0)
        cols_ref[at, :] = jnp.concatenate([cum, step[:, at], entry, gain], 0).T
        high = entry.astype(BF16).astype(F32)
        entries_ref[at, :] = jnp.concatenate([high, entry - high, blank], 0).T.astype(BF16)

    zero = jnp.zeros((8, TILE), F32)
    down_ref[2 * PAIR :] = zero
    up_ref[PAIR:] = zero
    for place, ref, start in ((6, down_ref, 0), (4, down_ref, PAIR), (2, up_ref, 0)):
        weigh_group(lax.rem(place + along(pos), RING), dy_ref, entries_ref, weighted)
        grad = dot(turned[TILE:, :], weighted[...])
        ref[start : start + TILE] = grad[:, :TILE]
        ref[start + TILE : start + PAIR] = grad[:, TILE:]


def first_grads(pos, dy, c, step, rate, gain):
    tokens, width = dy.shape
    state = c.shape[1]
    heads = step.shape[0]
    shape = jax.ShapeDtypeStruct
    return pl.pallas_call(
        first_grads_kernel,
        in_specs=[SMEM] + [VMEM] * 5,
        out_specs=(VMEM,) * 6,
        scratch_shapes=[pltpu.VMEM((tokens, width // RING), BF16)],
        out_shape=(
            shape((2 * PAIR + 8, TILE), F32), shape((PAIR + 8, TILE), F32),
            shape((tokens, TILE), F32), shape((heads, tokens), F32),
            shape((state, tokens), BF16), shape((tokens, TILE), BF16),
        ),
        compiler_params=params(),
        cost_estimate=pl.CostEstimate(
            flops=tokens * width * state, bytes_accessed=4 << 20, transcendentals=0
        ),
        name="first_grads",
    )(pos, dy, c, step, rate, gain)


def other_grads_kernel(
    pos, dy_ref, x_ref, turned, entries_ref, send_ref, keep_ref, far_ref, rest_ref,
    weighted, pairs,
):
    even = is_even(pos)
    length = pos[2]
    tokens, width = weighted.shape

    def group_of_heads(ahead, carry):
        group = lax.rem(ahead + along(pos), RING)
        weigh_group(group, dy_ref, entries_ref, weighted)
        gains = [jnp.zeros((1, TILE), F32)] * 2
        for block in range(tokens // TILE):
            at = slice(block * TILE, (block + 1) * TILE)
            live = iota((TILE, TILE), 0) + block * TILE < length
            for part in range(2):
                tile = pl.ds(pl.multiple_of((2 * group + part) * TILE, TILE), TILE)
                product = dy_ref[at, tile].astype(F32) * x_ref[at, tile].astype(F32)
                product = jnp.where(live, product, 0.0)
                gains[part] = gains[part] + jnp.sum(product, 0, keepdims=True)
        grad = dot(turned[...], weighted[...])
        first, second = grad[:, :TILE], grad[:, TILE:]
        keep_ref[ahead, :TILE] = jnp.where(even, first[:TILE], second[:TILE])
        send_ref[ahead, :TILE] = jnp.where(even, second[:TILE], first[:TILE])
        gains = [jnp.broadcast_to(gain, (8, TILE)) for gain in gains]
        keep_ref[ahead, TILE:] = jnp.where(even, gains[0], gains[1])
        send_ref[ahead, TILE:] = jnp.where(even, gains[1], gains[0])
        pairs[ahead, :TILE] = first[TILE:]
        pairs[ahead, TILE:] = second[TILE:]
        return carry

    lax.fori_loop(0, RING, group_of_heads, 0)
    far_ref[:PAIR] = pairs[3]
    far_ref[PAIR:] = jnp.zeros((8, TILE), F32)
    for slot, place in enumerate(KEPT):
        rest_ref[slot] = pairs[place]


def other_grads(pos, dy, x, turned, entries):
    tokens, width = dy.shape
    shapes = (
        (RING, TILE + 8, TILE), (RING, TILE + 8, TILE), (PAIR + 8, TILE), (len(KEPT), PAIR, TILE),
    )
    return pl.pallas_call(
        other_grads_kernel,
        in_specs=[SMEM] + [VMEM] * 4,
        out_specs=(VMEM,) * len(shapes),
        scratch_shapes=[
            pltpu.VMEM((tokens, width // RING), BF16),
            pltpu.VMEM((RING, PAIR, TILE), F32),
        ],
        out_shape=tuple(jax.ShapeDtypeStruct(shape, F32) for shape in shapes),
        compiler_params=params(),
        cost_estimate=pl.CostEstimate(
            flops=2 * tokens * width * 256, bytes_accessed=8 << 20, transcendentals=0
        ),
        name="other_grads",
    )(pos, dy, x, turned, entries)


def small(kernel, name, shapes, pos, *operands, nbytes=2 << 20):
    return pl.pallas_call(
        kernel,
        out_shape=tuple(jax.ShapeDtypeStruct(shape, F32) for shape in shapes),
        in_specs=[SMEM] + [VMEM] * len(operands),
        out_specs=(VMEM,) * len(shapes),
        compiler_params=params(),
        cost_estimate=pl.CostEstimate(flops=10**6, bytes_accessed=nbytes, transcendentals=0),
        name=name,
    )(pos, *operands)


def pass_on_totals_kernel(pos, rest_ref, down_ref, up_ref, total_ref, near_ref, far_ref, above_ref):
    near_ref[:PAIR] = rest_ref[3] + down_ref[:PAIR]
    near_ref[PAIR:] = down_ref[2 * PAIR :]
    far_ref[:PAIR] = rest_ref[2] + down_ref[PAIR : 2 * PAIR]
    far_ref[PAIR : PAIR + 8] = total_ref[...]
    far_ref[PAIR + 8 :] = down_ref[2 * PAIR :]
    above_ref[:PAIR] = rest_ref[1] + up_ref[:PAIR]
    above_ref[PAIR:] = up_ref[PAIR:]


def pass_on_totals(pos, *operands):
    shapes = ((PAIR + 8, TILE), (PAIR + 16, TILE), (PAIR + 8, TILE))
    return small(pass_on_totals_kernel, "pass_on_totals", shapes, pos, *operands)


def gather_totals_kernel(
    pos, rest_ref, far_up_ref, near_ref, far_ref, above_ref, down_ref, up_ref, mine_ref, other_ref,
    own_ref, send_ref, fade_ref,
):
    even = is_even(pos)
    pair = rest_ref[0] + far_up_ref[:PAIR] + near_ref[:PAIR] + far_ref[:PAIR] + above_ref[:PAIR]
    own_ref[...] = jnp.where(even, pair[:TILE], pair[TILE:])
    send_ref[...] = jnp.where(even, pair[TILE:], pair[:TILE])
    totals = {
        1: down_ref[2 * PAIR :], 2: near_ref[PAIR:], 3: far_ref[PAIR : PAIR + 8],
        4: far_ref[PAIR + 8 :], 5: far_up_ref[PAIR:], 6: above_ref[PAIR:], 7: up_ref[PAIR:],
    }
    later = jnp.zeros((8, TILE), F32)
    for ahead, total in totals.items():
        later = later + jnp.where(along(pos) + ahead < RING, total, 0.0)
    fade_ref[0] = jnp.exp(later + jnp.where(even, other_ref[...], 0.0))
    fade_ref[1] = jnp.exp(later + jnp.where(even, 0.0, mine_ref[...]))


def gather_totals(pos, *operands):
    shapes = ((TILE, TILE), (TILE, TILE), (2, 8, TILE))
    return small(gather_totals_kernel, "gather_totals", shapes, pos, *operands)


def contrib_kernel(
    pos, own_ref, got_ref, b_ref, fade_ref, keep_ref, came_ref, down_ref, up_ref, far_ref, rest_ref
):
    state = b_ref.shape[1]
    turned = b_ref[...].astype(F32).T.astype(BF16)
    turned_got = jnp.concatenate([got_ref[RING].T, got_ref[RING + 1].T], 0).astype(BF16)
    low = iota((8, TILE), 1) < HALF
    refs = {6: down_ref.at[0], 4: down_ref.at[1], 2: up_ref, 3: far_ref}
    refs.update({place: rest_ref.at[slot] for slot, place in enumerate(KEPT)})
    for ahead, ref in refs.items():
        place = lax.rem(along(pos) + ahead, RING)
        shift = lax.rem(2 * TILE - 32 - 4 * place - 2 * (pos[0] & 1), TILE)
        scales = [spread(pltpu.roll(fade_ref[k], shift, 1), 0, low)[:1] for k in range(2)]
        own = dot(turned, own_ref[place])
        got = dot(turned_got, got_ref[place].astype(BF16))
        ref[:state] = own * scales[0] + got * scales[1]
        ref[state:] = keep_ref[ahead] + came_ref[ahead]


def contributions(pos, *operands):
    shapes = ((2, FULL, TILE), (FULL, TILE), (FULL, TILE), (len(KEPT), FULL, TILE))
    return small(contrib_kernel, "contributions", shapes, pos, *operands, nbytes=6 << 20)


def pass_on_kernel(pos, rest_ref, down_ref, up_ref, near_ref, far_ref, above_ref):
    near_ref[...] = rest_ref[3] + down_ref[0]
    far_ref[...] = rest_ref[2] + down_ref[1]
    above_ref[...] = rest_ref[1] + up_ref[...]


def pass_on(pos, *operands):
    return small(pass_on_kernel, "pass_on", ((FULL, TILE),) * 3, pos, *operands)


def share_kernel(
    pos, rest_ref, far_up_ref, near_ref, far_ref, above_ref, own_ref, got_ref, share_ref
):
    share_ref[:FULL] = rest_ref[0] + far_up_ref[...] + near_ref[...] + far_ref[...] + above_ref[...]
    share_ref[FULL:] = own_ref[...] + got_ref[...]


def make_share(pos, *operands):
    return small(share_kernel, "make_share", ((FULL + TILE, TILE),), pos, *operands)[0]


def choose_kernel(pos, first, second, third, fourth, message_ref, lower_ref):
    here = pos[1]
    distance_to_start = (here - pos[3 + here]) & 3
    shares = (first, second, third, fourth)
    start = first[:PAIR]
    upper, lower = jnp.zeros((TILE, TILE), F32), jnp.zeros((TILE, TILE), F32)
    gains = jnp.zeros((8, TILE), F32)
    for distance, ref in enumerate(shares):
        start = jnp.where(distance_to_start == distance, ref[:PAIR], start)
        mine = pos[3 + ((here - distance) & 3)] == here
        upper = upper + jnp.where(mine, ref[PAIR : PAIR + TILE], 0.0)
        lower = lower + jnp.where(mine, ref[FULL:], 0.0)
        gains = gains + ref[PAIR + TILE : FULL]
    message_ref[:UPPER] = start[:UPPER]
    message_ref[UPPER : UPPER + TILE] = upper
    message_ref[UPPER + TILE : UPPER + PAIR] = lower
    message_ref[UPPER + PAIR :] = gains
    lower_ref[...] = start[UPPER:]


def choose(pos, *operands):
    shapes = ((MESSAGE, TILE), (PAIR - UPPER, TILE))
    return small(choose_kernel, "choose", shapes, pos, *operands)


def prepare_kernel(b_ref, c_ref, scores, scores_t, b_turned, c_turned):
    square = (TILE, TILE)
    upper = iota(square, 0) <= iota(square, 1)
    lower = iota(square, 0) >= iota(square, 1)
    for block in range(scores.shape[0]):
        at = slice(block * TILE, (block + 1) * TILE)
        b_rows, c_rows = b_ref[at, :], c_ref[at, :]
        scores[block] = jnp.where(lower, dot(c_rows, b_rows, ((1,), (1,))), 0.0)
        scores_t[block] = jnp.where(upper, dot(b_rows, c_rows, ((1,), (1,))), 0.0)
        b_turned[:, at] = b_rows.astype(F32).T.astype(BF16)
        c_turned[:, at] = c_rows.astype(F32).T.astype(BF16)


def prepare(b, c):
    tokens, state = b.shape
    square = jax.ShapeDtypeStruct((tokens // TILE, TILE, TILE), F32)
    turned = jax.ShapeDtypeStruct((state, tokens), BF16)
    return pl.pallas_call(
        prepare_kernel,
        out_shape=(square, square, turned, turned),
        in_specs=[VMEM, VMEM],
        out_specs=(VMEM,) * 4,
        compiler_params=params(),
        cost_estimate=pl.CostEstimate(flops=10**8, bytes_accessed=2 << 20, transcendentals=0),
        name="prepare",
    )(b, c)


def mix_kernel(
    group, pos, x_ref, dy_ref, b_ref, c_ref, cols_ref, rows_ref,
    scores, scores_t, b_turned, c_turned, *rest
):
    (
        y_hbm, dx_hbm, y_ref, dx_ref, inner_dx, out_scale, wdy, state, ends, left,
    ) = rest[-10:]
    length = pos[2]
    tokens, width = y_ref.shape
    blocks = tokens // TILE
    square = (TILE, TILE)
    ours = pl.ds(group * width, width)

    low = iota(square, 1) < HALF

    def split(value):
        return jnp.concatenate(
            [jnp.where(low, value, 0.0), jnp.where(low, 0.0, value)], 0
        ).astype(BF16)

    state[...] = jnp.zeros_like(state)

    for block in range(blocks):
        at = slice(block * TILE, (block + 1) * TILE)
        cols = pltpu.roll(cols_ref[at, :], (TILE - 4 * group) % TILE, 1)
        live = iota(square, 0) + block * TILE < length
        rows = rows_ref[group // 2 * 8 : group // 2 * 8 + 8, at]
        rows = rows[4 * (group % 2) : 4 * (group % 2) + 4]
        held = state[...]
        carried = dot(c_ref[at, :], held.astype(BF16))
        update, end = [], []
        for part in range(2):
            lanes = slice(part * TILE, (part + 1) * TILE)
            tile = slice(group * width + part * TILE, group * width + (part + 1) * TILE)
            x = x_ref[at, tile].astype(F32)
            dy = jnp.where(live, dy_ref[at, tile].astype(F32), 0.0)
            gain = spread(cols[:8], 96 + 2 * part, low[:8])[:1]
            sides = [
                jnp.broadcast_to(cols[:, 2 * part + k : 2 * part + k + 1], square)
                for k in range(2)
            ]
            step = spread(cols, 32 + 2 * part, low)
            log = jnp.where(low, sides[0], sides[1])
            last = log[TILE - 1 :]
            since = jnp.exp2(log)
            until = jnp.exp2(last - log)
            ahead, back = [], []
            for k in range(2):
                gap = sides[k] - rows[2 * part + k : 2 * part + k + 1]
                ahead.append((jnp.exp2(jnp.minimum(gap, 0.0)) * scores[block]).astype(BF16))
                back.append((jnp.exp2(jnp.minimum(-gap, 0.0)) * scores_t[block]).astype(BF16))
            stepped = x * step
            y = dot(jnp.concatenate(ahead, 1), split(stepped)) + gain * x
            y = y + since * carried[:, lanes]
            y_ref[at, lanes] = jnp.where(live, y, 0.0)
            dx = dot(jnp.concatenate(back, 1), split(dy))
            inner_dx[at, lanes] = step * dx + gain * dy
            out_scale[at, lanes] = step * until
            wdy[at, lanes] = (dy * since).astype(BF16)
            update.append((stepped * until).astype(BF16))
            end.append(jnp.exp2(last))
        end = jnp.concatenate(end, 1)
        ends[block] = jnp.broadcast_to(end, ends.shape[1:])
        state[...] = end * held + dot(b_turned[:, at], jnp.concatenate(update, 1))

    out_y = pltpu.make_async_copy(y_ref, y_hbm.at[group], left.at[0])
    out_y.start()
    state[...] = jnp.zeros_like(state)

    for block in reversed(range(blocks)):
        at = slice(block * TILE, (block + 1) * TILE)
        held = state[...]
        dx = inner_dx[at, :] + out_scale[at, :] * dot(b_ref[at, :], held.astype(BF16))
        dx_ref[at, :] = dx.astype(BF16)
        state[...] = ends[block][:1] * held + dot(c_turned[:, at], wdy[at, :])

    out_dx = pltpu.make_async_copy(dx_ref, dx_hbm.at[:, ours], left.at[1])
    out_dx.start()
    out_y.wait()
    out_dx.wait()


def mix(group, pos, x, dy, b, c, cols, rows, prepared, before):
    tokens, total = x.shape
    state = b.shape[1]
    width = total // RING
    blocks = tokens // TILE
    operands = [pos, x, dy, b, c, cols, rows, *prepared]
    specs = [SMEM] + [VMEM] * (len(operands) - 1)
    alias = {}
    if before is not None:
        alias = {len(operands): 0, len(operands) + 1: 1}
        specs += [HBM, HBM]
        operands += list(before)
    return pl.pallas_call(
        functools.partial(mix_kernel, group),
        out_shape=(
            jax.ShapeDtypeStruct((RING, tokens, width), F32),
            jax.ShapeDtypeStruct((tokens, total), BF16),
        ),
        in_specs=specs,
        out_specs=(HBM, HBM),
        scratch_shapes=[
            pltpu.VMEM((tokens, width), F32),
            pltpu.VMEM((tokens, width), BF16),
            pltpu.VMEM((tokens, width), F32),
            pltpu.VMEM((tokens, width), F32),
            pltpu.VMEM((tokens, width), BF16),
            pltpu.VMEM((state, width), F32),
            pltpu.VMEM((blocks, 8, width), F32),
            pltpu.SemaphoreType.DMA((2,)),
        ],
        input_output_aliases=alias,
        compiler_params=params(),
        cost_estimate=pl.CostEstimate(
            flops=8 * tokens * width * state, bytes_accessed=4 << 20, transcendentals=0
        ),
        name="mix",
    )(*operands)


def finish_kernel(
    pos, c_ref, entries_ref, y_hbm, own_ref, got_ref, p0, p1, p7, p3, p5, p24, p6, out_hbm,
    state, y_all, out_all, arrived, left,
):
    even = is_even(pos)
    tokens, width = out_all.shape[1:]

    def store(place):
        start = pl.multiple_of(lax.rem(place + along(pos), RING) * width, width)
        target = out_hbm.at[:, pl.ds(start, width)]
        return pltpu.make_async_copy(out_all.at[place], target, left.at[place])

    def load(place):
        source = y_hbm.at[lax.rem(place + along(pos), RING)]
        return pltpu.make_async_copy(source, y_all.at[place], arrived.at[place])

    for place in range(RING):
        load(place).start()

    at = slice(TILE + 8, TILE + 8 + UPPER)
    for place, ref in enumerate((p0, p1, p24.at[0], p3, p24.at[1], p5, p6, p7)):
        own, got = own_ref[place, at], got_ref[place, at]
        state[place, :UPPER, :TILE] = jnp.where(even, own, got).astype(BF16)
        state[place, :UPPER, TILE:] = jnp.where(even, got, own).astype(BF16)
        state[place, UPPER:, :TILE] = ref[0].astype(BF16)
        state[place, UPPER:, TILE:] = ref[1].astype(BF16)

    def group_of_heads(ahead, carry):
        group = lax.rem(ahead + along(pos), RING)
        scale = scale_of(group, entries_ref, width)
        carried = scale * dot(c_ref[...], state[ahead])
        load(ahead).wait()
        y = y_all[ahead] + carried
        out_all[ahead] = y.astype(BF16)
        store(ahead).start()
        return carry

    lax.fori_loop(0, RING, group_of_heads, 0)
    for place in range(RING):
        store(place).wait()


def finish(pos, c, entries, y, own, got, pairs):
    _, tokens, width = y.shape
    return pl.pallas_call(
        finish_kernel,
        in_specs=[SMEM, VMEM, VMEM, HBM, VMEM, VMEM] + [VMEM] * len(pairs),
        out_specs=HBM,
        scratch_shapes=[
            pltpu.VMEM((RING, 2 * TILE, width), BF16),
            pltpu.VMEM((RING, tokens, width), F32),
            pltpu.VMEM((RING, tokens, width), BF16),
            pltpu.SemaphoreType.DMA((RING,)),
            pltpu.SemaphoreType.DMA((RING,)),
        ],
        out_shape=jax.ShapeDtypeStruct((tokens, RING * width), BF16),
        compiler_params=params(58),
        cost_estimate=pl.CostEstimate(
            flops=2 * tokens * width * RING * 256, bytes_accessed=10 << 20, transcendentals=0
        ),
        name="finish",
    )(pos, c, entries, y, own, got, *pairs)


def back_kernel(pos, b_ref, got_ref, p0, p1, p7, p3, p5, p24, p6, own_ref, send_ref):
    mine = b_ref[...]
    other = jnp.concatenate([got_ref[RING], got_ref[RING + 1]], 1).astype(BF16)
    for place, ref in enumerate((p0, p1, p24.at[0], p3, p24.at[1], p5, p6, p7)):
        grad = ref[UPPER : UPPER + PAIR].astype(BF16)
        own_ref[place] = dot(mine, grad)
        send_ref[place, :TILE] = dot(other, grad)
        send_ref[place, TILE : TILE + 8] = ref[UPPER + PAIR :]
        send_ref[place, TILE + 8 :] = ref[:UPPER]


def back(pos, *operands):
    shapes = ((RING, TILE, TILE), (RING, TILE + 8 + UPPER, TILE))
    return small(back_kernel, "back", shapes, pos, *operands, nbytes=4 << 20)


def prompt_dx_kernel(
    pos, own_ref, sent_ref, got_ref, cols_ref, fade_ref, out_hbm, skip_ref, out_all, left
):
    even = is_even(pos)
    low = iota((TILE, TILE), 1) < HALF
    scale = cols_ref[...] * pltpu.roll(fade_ref[0], TILE - 32, 1)[:1]
    width = out_all.shape[2]

    def store(place):
        start = pl.multiple_of(lax.rem(place + along(pos), RING) * width, width)
        target = out_hbm.at[:, pl.ds(start, width)]
        return pltpu.make_async_copy(out_all.at[place], target, left.at[place])

    def group_of_heads(ahead, carry):
        group = lax.rem(ahead + along(pos), RING)
        cols = pltpu.roll(scale, lax.rem(TILE - 4 * group, TILE), 1)
        own, got = own_ref[ahead], got_ref[ahead, :TILE]
        tiles = (jnp.where(even, own, got), jnp.where(even, got, own))
        for part in range(2):
            lanes = slice(part * TILE, (part + 1) * TILE)
            out_all[ahead, :, lanes] = (tiles[part] * spread(cols, 2 * part, low)).astype(BF16)
        store(ahead).start()
        own, got = sent_ref[ahead, TILE : TILE + 8], got_ref[ahead, TILE : TILE + 8]
        skip_ref[group, 0] = jnp.where(even, own, got)
        skip_ref[group, 1] = jnp.where(even, got, own)
        return carry

    lax.fori_loop(0, RING, group_of_heads, 0)
    for place in range(RING):
        store(place).wait()


def prompt_gradient(pos, own, sent, got, cols, fade):
    return pl.pallas_call(
        prompt_dx_kernel,
        in_specs=[SMEM] + [VMEM] * 5,
        out_specs=(HBM, VMEM),
        scratch_shapes=[
            pltpu.VMEM((RING, TILE, 2 * TILE), BF16),
            pltpu.SemaphoreType.DMA((RING,)),
        ],
        out_shape=(
            jax.ShapeDtypeStruct((TILE, RING * 2 * TILE), BF16),
            jax.ShapeDtypeStruct((RING, 2, 8, TILE), F32),
        ),
        compiler_params=params(),
        cost_estimate=pl.CostEstimate(flops=10**6, bytes_accessed=2 << 20, transcendentals=0),
        name="prompt_gradient",
    )(pos, own, sent, got, cols, fade)


def along_z(value, distance):
    pairs = [
        (2 * z + y, 2 * ((z + distance) % RING) + y) for z in range(RING) for y in range(2)
    ]
    return lax.ppermute(value, "sample", pairs)


def swap(value):
    return lax.ppermute(value, "sample", [(s, s ^ 1) for s in range(2 * RING)])


def along_dp(value, distance):
    return lax.ppermute(value, "dp", [(i, (i + distance) % 4) for i in range(4)])


def together(*values):
    return lax.optimization_barrier(values)


def from_all(own, beside):
    one, seven = along_z(own, -1), along_z(own, 1)
    three, five = along_z(own, -3), along_z(own, 3)
    one, seven, three, five, beside = together(one, seven, three, five, beside)
    both = along_z(jnp.stack([one, three]), -1)
    six = along_z(seven, 1)
    return [own, one, seven, three, five, both, six], beside


def body(
    prompt_x, prompt_b, prompt_step, resp_x, resp_b, resp_c, resp_step,
    decay_rate, skip_gain, lengths, prompt_map, resp_cotangent,
):
    place = lax.axis_index("sample")
    here = lax.axis_index("dp")
    pos = jnp.concatenate(
        [place[None].astype(jnp.int32), here[None].astype(jnp.int32), lengths[0], prompt_map]
    )
    rate, gain = decay_rate[None], skip_gain[None]
    x, dy, b, c = resp_x[0, 0], resp_cotangent[0, 0], resp_b[0, 0], resp_c[0, 0]

    mine = sum_logs(prompt_step[0], rate)
    other = swap(mine)
    dy_first, _ = together(dy, mine)

    down, up, cols, rows, turned, entries = first_grads(
        pos, dy_first, c, resp_step[0, 0], rate, gain
    )
    total = mine + other
    down = lax.dynamic_update_slice(down, total, (2 * PAIR, 0))
    up = lax.dynamic_update_slice(up, total, (PAIR, 0))

    prompt_ready, _ = together(prompt_x[0], down)
    sent, own, coef = weigh(pos, prompt_ready, prompt_b[0], prompt_step[0], rate)
    got = swap(sent)
    down, up = along_z(down, -1), along_z(up, 1)

    entries, _ = together(entries, sent)
    upper, kept, far, rest = other_grads(pos, dy, x, turned, entries)
    far_up = lax.dynamic_update_slice(far, total, (PAIR, 0))

    b_ready, _ = together(b, rest)
    prepared = prepare(b_ready, c)
    groups = iter(range(RING))

    def within(before, after, count=2):
        for _ in range(count):
            ready, _ = together(x, after)
            before = mix(next(groups), pos, ready, dy, b, c, cols, rows, prepared, before)
        return before

    near, far, above = pass_on_totals(pos, rest, down, up, total)
    near, far, above, far_up, got, upper = together(near, far, above, far_up, got, upper)
    came = swap(upper)
    mixed = within(None, near)
    near, far, above = along_z(near, -1), along_z(far, -3), along_z(above, 1)
    far_up = along_z(far_up, 3)
    rest, mixed = together(rest, mixed)
    low_own, low_send, fade = gather_totals(
        pos, rest, far_up, near, far, above, down, up, mine, other
    )
    low_got = swap(low_send)

    down, up, far_up, rest = contributions(pos, own, got, prompt_b[0], fade, kept, came)
    down, up = along_z(down, -1), along_z(up, 1)
    mixed = within(mixed, rest)
    rest, mixed = together(rest, mixed)
    near, far, above = pass_on(pos, rest, down, up)
    mixed = within(mixed, near)
    near, far, above, far_up = together(near, far, above, far_up)
    near, far, above = along_z(near, -1), along_z(far, -3), along_z(above, 1)
    far_up = along_z(far_up, 3)
    rest, mixed = together(rest, mixed)
    share = make_share(pos, rest, far_up, near, far, above, low_own, low_got)

    others = [along_dp(share, d) for d in (1, 2, 3)]
    mixed = within(mixed, share)
    share, mixed = together(share, mixed)
    message, lower = choose(pos, share, *others)

    lower_got = swap(lower)
    pieces, lower_got = from_all(message, lower_got)
    own_dx, sent = back(pos, prompt_b[0], got, *pieces)
    got_last = swap(sent)
    even = place & 1 == 0
    pair = jnp.stack([jnp.where(even, lower, lower_got), jnp.where(even, lower_got, lower)])
    pair, _ = together(pair, sent)
    pairs, _ = from_all(pair, pair)
    prompt_dx, skip = prompt_gradient(pos, own_dx, sent, got_last, coef, fade)
    skip_grad = jnp.sum(skip[:, :, 0].reshape(-1, HALF), 1)
    resp_y = finish(pos, c, entries, mixed[0], sent, got_last, pairs)
    return (resp_y[None, None], mixed[1][None, None], prompt_dx[None], skip_grad)


def solution(mesh):
    placed = (
        P("dp", "sample", "tensor"),
        P("dp", "sample", None),
        P("dp", "tensor", "sample"),
        P("dp", "sample", None, "tensor"),
        P("dp", "sample", None, None),
        P("dp", "sample", None, None),
        P("dp", "sample", "tensor", None),
        P("tensor"),
        P("tensor"),
        P("dp", "sample"),
        P(),
        P("dp", "sample", None, "tensor"),
    )
    return jax.shard_map(
        body,
        mesh=mesh,
        in_specs=placed,
        out_specs=(
            P("dp", "sample", None, "tensor"),
            P("dp", "sample", None, "tensor"),
            P("dp", "sample", "tensor"),
            P("tensor"),
        ),
        check_vma=False,
    )
```

```python
import functools

import jax
import jax.numpy as jnp
from jax import lax
from jax.experimental import pallas as pl
from jax.experimental.pallas import tpu as pltpu
from jax.sharding import PartitionSpec as P

F32 = jnp.float32
BF16 = jnp.bfloat16
LOG2E = 1.4426950408889634
EXACT = lax.Precision.HIGHEST
TILE = 128
HALF = 64
RING = 8
STATE = 2 * TILE
PAIR = 2 * STATE
FULL = STATE + 8
KEPT = (0, 1, 3, 5, 7)
VMEM = pl.BlockSpec(memory_space=pltpu.VMEM)
SMEM = pl.BlockSpec(memory_space=pltpu.SMEM)
HBM = pl.BlockSpec(memory_space=pltpu.HBM)


def dot(left, right, dims=((1,), (0,)), precision=None):
    return lax.dot_general(
        left, right, (dims, ((), ())), precision=precision, preferred_element_type=F32
    )


def iota(shape, axis):
    return lax.broadcasted_iota(jnp.int32, shape, axis)


def along(pos):
    return pos[0] >> 1


def is_even(pos):
    return pos[0] & 1 == 0


def column(row):
    heads = row.shape[1]
    square = (heads, heads)
    return jnp.sum(jnp.where(iota(square, 0) == iota(square, 1), row, 0.0), 1, keepdims=True)


def params(megabytes=14):
    return pltpu.CompilerParams(vmem_limit_bytes=megabytes << 20)


def spread(cols, first, low):
    return jnp.where(low, cols[:, first : first + 1], cols[:, first + 1 : first + 2])


def sum_logs_kernel(step_ref, rate_ref, out_ref):
    log = -(step_ref[...] * column(rate_ref[...]))
    heads = log.shape[0]
    total = dot(jnp.ones((8, TILE), F32), log, ((1,), (1,)), EXACT)
    blank = jnp.zeros((8, TILE - 2 * heads), F32)
    out_ref[...] = jnp.concatenate([jnp.zeros((8, heads), F32), total, blank], 1)


def sum_logs(step, rate):
    return pl.pallas_call(
        sum_logs_kernel,
        out_shape=jax.ShapeDtypeStruct((8, TILE), F32),
        in_specs=[VMEM, VMEM],
        out_specs=VMEM,
        compiler_params=params(61),
        cost_estimate=pl.CostEstimate(flops=10**5, bytes_accessed=1 << 15, transcendentals=0),
        name="sum_logs",
    )(step, rate)


def scale_of(group, entries_ref, width):
    head = 4 * group + iota((TILE, width), 1) // HALF
    row = iota((TILE, width), 0)
    chosen = (row < 64) & (row % 32 == head)
    return dot(entries_ref[...], chosen.astype(F32).astype(BF16))


def weigh_group(group, dy, entries_ref, weighted):
    scale = scale_of(group, entries_ref, weighted.shape[1])
    weighted[...] = (dy.astype(F32) * scale).astype(BF16)


FIRST = (6, 2, 4)


def begin_kernel(
    pos, *refs
):
    sources, rest = refs[:8], refs[8:]
    (sent_ref, own_ref, coef_ref, down_ref, up_ref, cols_ref, rows_ref, turned,
     entries_ref) = rest[:9]
    targets, (dy_ref, weighted, arrived) = rest[9:16], rest[16:]
    even = is_even(pos)
    length = pos[2]
    tokens, width = weighted.shape
    groups = [lax.rem(place + along(pos), RING) for place in FIRST]
    copies = [
        pltpu.make_async_copy(source, target, arrived.at[index])
        for index, (source, target) in enumerate(zip(sources, targets))
    ]
    for index, group in enumerate(groups):
        at = pl.ds(pl.multiple_of(group * width, width), width)
        copies.append(
            pltpu.make_async_copy(sources[7].at[:, at], dy_ref.at[index], arrived.at[7 + index])
        )
    for copy in copies:
        copy.start()
    for copy in copies[:5]:
        copy.wait()
    ps_ref, rate_ref, gain_ref, pb_ref, px_ref, step_ref, c_ref = targets

    square = (TILE, TILE)
    rate = column(rate_ref[...])
    step = ps_ref[...]
    heads = step.shape[0]
    log = -(step * rate)
    later = (iota(square, 0) > iota(square, 1)).astype(F32)
    coef = jnp.exp(dot(log, later, precision=EXACT)) * step
    cols = jnp.concatenate([coef, jnp.zeros((TILE - heads, TILE), F32)], 0).T
    coef_ref[...] = cols
    low = iota(square, 1) < HALF
    for place in range(RING):
        pair = []
        for part in range(2):
            tile = 2 * place + part
            x = px_ref[:, tile * TILE : (tile + 1) * TILE].astype(F32)
            pair.append(x * spread(cols, 2 * tile, low))
        own_ref[place] = jnp.where(even, pair[0], pair[1]).astype(BF16)
        sent_ref[place] = jnp.where(even, pair[1], pair[0]).astype(BF16).astype(F32)
    sent_ref[RING] = pb_ref[:, :TILE].astype(F32)
    sent_ref[RING + 1] = pb_ref[:, TILE:].astype(F32)

    copies[5].wait()
    copies[6].wait()
    step = step_ref[...]
    log = step * rate * (-LOG2E)
    gain = jnp.broadcast_to(column(gain_ref[...]), (heads, TILE))
    upto = (iota(square, 0) <= iota(square, 1)).astype(F32)
    run = jnp.zeros((heads, 1), F32)
    blank = jnp.zeros((TILE - 2 * heads, TILE), F32)
    for block in range(tokens // TILE):
        at = slice(block * TILE, (block + 1) * TILE)
        turned[:, at] = c_ref[at, :].astype(F32).T.astype(BF16)
        cum = dot(log[:, at], upto, precision=EXACT)
        rows_ref[:, at] = cum
        whole = cum + run
        run = whole[:, TILE - 1 :]
        live = iota((heads, TILE), 1) + block * TILE < length
        entry = jnp.where(live, jnp.exp2(whole), 0.0)
        cols_ref[at, :] = jnp.concatenate([cum, step[:, at], entry, gain], 0).T
        high = entry.astype(BF16).astype(F32)
        entries_ref[at, :] = jnp.concatenate([high, entry - high, blank], 0).T.astype(BF16)

    for index, group in enumerate(groups):
        copies[7 + index].wait()
        weigh_group(group, dy_ref[index], entries_ref, weighted)
        grad = dot(turned[...], weighted[...])
        if FIRST[index] == 4:
            down_ref[PAIR:] = grad[:, :TILE]
            up_ref[PAIR:] = grad[:, TILE:]
        else:
            ref = down_ref if FIRST[index] == 6 else up_ref
            ref[:STATE] = grad[:, :TILE]
            ref[STATE:PAIR] = grad[:, TILE:]


def begin(pos, ps, rate, gain, pb, px, step, c, dy):
    tokens, width = dy.shape
    state = c.shape[1]
    heads = step.shape[0]
    shape = jax.ShapeDtypeStruct
    small_ones = (ps, rate, gain, pb, px, step, c)
    return pl.pallas_call(
        begin_kernel,
        in_specs=[SMEM] + [HBM] * 8,
        out_specs=(VMEM,) * 9,
        scratch_shapes=[pltpu.VMEM(operand.shape, operand.dtype) for operand in small_ones]
        + [
            pltpu.VMEM((len(FIRST), tokens, width // RING), BF16),
            pltpu.VMEM((tokens, width // RING), BF16),
            pltpu.SemaphoreType.DMA((7 + len(FIRST),)),
        ],
        out_shape=(
            shape((RING + 2, TILE, TILE), F32), shape((RING, TILE, TILE), BF16),
            shape((TILE, TILE), F32),
            shape((PAIR + STATE, TILE), F32), shape((PAIR + STATE, TILE), F32),
            shape((tokens, TILE), F32), shape((heads, tokens), F32),
            shape((state, tokens), BF16), shape((tokens, TILE), BF16),
        ),
        compiler_params=params(60),
        cost_estimate=pl.CostEstimate(
            flops=tokens * width * state, bytes_accessed=4 << 20, transcendentals=0
        ),
        name="begin",
    )(pos, *small_ones, dy)


def other_grads_kernel(
    pos, dy_ref, x_ref, turned, entries_ref, rest_ref, send_ref, keep_ref, weighted
):
    even = is_even(pos)
    length = pos[2]
    tokens, width = weighted.shape

    def piece(slot, carry):
        ahead = jnp.where(slot < 1, 0, 2 * slot - 1)
        group = lax.rem(ahead + along(pos), RING)
        at = pl.ds(pl.multiple_of(group * width, width), width)
        weigh_group(group, dy_ref[:, at], entries_ref, weighted)
        grad = dot(turned[...], weighted[...])
        rest_ref[slot, :STATE] = grad[:, :TILE]
        rest_ref[slot, STATE:] = grad[:, TILE:]
        return carry

    def gain_of_group(ahead, carry):
        group = lax.rem(ahead + along(pos), RING)
        gains = [jnp.zeros((1, TILE), F32)] * 2
        for block in range(tokens // TILE):
            at = slice(block * TILE, (block + 1) * TILE)
            live = iota((TILE, TILE), 0) + block * TILE < length
            for part in range(2):
                tile = pl.ds(pl.multiple_of((2 * group + part) * TILE, TILE), TILE)
                product = dy_ref[at, tile].astype(F32) * x_ref[at, tile].astype(F32)
                product = jnp.where(live, product, 0.0)
                gains[part] = gains[part] + jnp.sum(product, 0, keepdims=True)
        gains = [jnp.broadcast_to(gain, (8, TILE)) for gain in gains]
        keep_ref[ahead] = jnp.where(even, gains[0], gains[1])
        send_ref[ahead] = jnp.where(even, gains[1], gains[0])
        return carry

    lax.fori_loop(0, len(KEPT), piece, 0)
    lax.fori_loop(0, RING, gain_of_group, 0)


def other_grads(pos, dy, x, turned, entries):
    tokens, width = dy.shape
    shapes = ((len(KEPT), PAIR, TILE), (RING, 8, TILE), (RING, 8, TILE))
    return pl.pallas_call(
        other_grads_kernel,
        in_specs=[SMEM] + [VMEM] * 4,
        out_specs=(VMEM,) * len(shapes),
        scratch_shapes=[pltpu.VMEM((tokens, width // RING), BF16)],
        out_shape=tuple(jax.ShapeDtypeStruct(shape, F32) for shape in shapes),
        compiler_params=params(),
        cost_estimate=pl.CostEstimate(
            flops=2 * tokens * width * 256, bytes_accessed=8 << 20, transcendentals=0
        ),
        name="other_grads",
    )(pos, dy, x, turned, entries)


def small(kernel, name, shapes, pos, *operands, nbytes=2 << 20):
    return pl.pallas_call(
        kernel,
        out_shape=tuple(jax.ShapeDtypeStruct(shape, F32) for shape in shapes),
        in_specs=[SMEM] + [VMEM] * len(operands),
        out_specs=(VMEM,) * len(shapes),
        compiler_params=params(),
        cost_estimate=pl.CostEstimate(flops=10**6, bytes_accessed=nbytes, transcendentals=0),
        name=name,
    )(pos, *operands)


def half(rows):
    return rows // 16 * 8 + rows % 16


def pass_first_kernel(pos, rest_ref, down_ref, up_ref, five_ref, three_ref):
    rows = five_ref.shape[0]
    cut = half(rows)
    five_ref[:cut] = rest_ref[3, :cut] + down_ref[rows:]
    five_ref[cut:] = rest_ref[3, cut:]
    three_ref[:cut] = rest_ref[2, :cut]
    three_ref[cut:] = rest_ref[2, cut:] + up_ref[rows:]


def pass_first(pos, rest, down, up):
    return small(pass_first_kernel, "pass_first", (rest.shape[1:],) * 2, pos, rest, down, up)


def pass_second_kernel(
    pos, rest_ref, down_ref, up_ref, far_down_ref, far_up_ref, seven_ref, one_ref
):
    rows = seven_ref.shape[0]
    seven_ref[...] = rest_ref[4] + down_ref[:rows] + far_down_ref[...]
    one_ref[...] = rest_ref[1] + up_ref[:rows] + far_up_ref[...]


def pass_second(pos, rest, *operands):
    shapes = (rest.shape[1:],) * 2
    return small(pass_second_kernel, "pass_second", shapes, pos, rest, *operands)


def own_tile_kernel(pos, rest_ref, down_ref, up_ref, own_ref, send_ref):
    even = is_even(pos)
    first, second = slice(0, STATE), slice(STATE, PAIR)
    first = rest_ref[0, first] + down_ref[first] + up_ref[first]
    second = rest_ref[0, second] + down_ref[second] + up_ref[second]
    own_ref[...] = jnp.where(even, first, second)
    send_ref[...] = jnp.where(even, second, first)


def own_tile(pos, *operands):
    return small(own_tile_kernel, "own_tile", ((STATE, TILE),) * 2, pos, *operands)


def contrib_kernel(
    pos, own_ref, got_ref, b_ref, after_ref, after_got_ref, keep_ref, came_ref,
    down_ref, up_ref, rest_ref, fade_ref,
):
    turned = b_ref[...].astype(F32).T.astype(BF16)
    turned_got = jnp.concatenate([got_ref[RING].T, got_ref[RING + 1].T], 0).astype(BF16)
    low = iota((8, TILE), 1) < HALF
    fades = (jnp.exp(after_ref[...]), jnp.exp(after_got_ref[...]))
    fade_ref[...] = fades[0]
    cut = half(FULL)
    for ahead in range(RING):
        place = lax.rem(along(pos) + ahead, RING)
        shift = lax.rem(2 * TILE - 32 - 4 * place - 2 * (pos[0] & 1), TILE)
        scales = [spread(pltpu.roll(fade, shift, 1), 0, low)[:1] for fade in fades]
        own = dot(turned, own_ref[place])
        got = dot(turned_got, got_ref[place].astype(BF16))
        piece = jnp.concatenate(
            [own * scales[0] + got * scales[1], keep_ref[ahead] + came_ref[ahead]], 0
        )
        if ahead == 4:
            down_ref[FULL:] = piece[:cut]
            up_ref[FULL:] = piece[cut:]
        elif ahead in KEPT:
            rest_ref[KEPT.index(ahead)] = piece
        else:
            ref = down_ref if ahead == 6 else up_ref
            ref[:FULL] = piece


def contributions(pos, *operands):
    cut = half(FULL)
    shapes = (
        (FULL + cut, TILE), (2 * FULL - cut, TILE), (len(KEPT), FULL, TILE), (8, TILE),
    )
    return small(contrib_kernel, "contributions", shapes, pos, *operands, nbytes=6 << 20)


def share_kernel(pos, rest_ref, down_ref, up_ref, own_ref, got_ref, share_ref):
    share_ref[:FULL] = rest_ref[0] + down_ref[...] + up_ref[...]
    share_ref[FULL:] = own_ref[...] + got_ref[...]


def make_share(pos, *operands):
    return small(share_kernel, "make_share", ((FULL + STATE, TILE),), pos, *operands)[0]


def choose_kernel(pos, first, second, third, fourth, message_ref, start_ref):
    here = pos[1]
    distance_to_start = (here - pos[3 + here]) & 3
    shares = (first, second, third, fourth)
    start = first[:STATE]
    grad = jnp.zeros((STATE, TILE), F32)
    gains = jnp.zeros((8, TILE), F32)
    for distance, ref in enumerate(shares):
        start = jnp.where(distance_to_start == distance, ref[:STATE], start)
        mine = pos[3 + ((here - distance) & 3)] == here
        grad = grad + jnp.where(mine, ref[FULL:], 0.0)
        gains = gains + ref[STATE:FULL]
    message_ref[:STATE] = grad
    message_ref[STATE:] = gains
    start_ref[...] = start


def choose(pos, *operands):
    shapes = ((FULL, TILE), (STATE, TILE))
    return small(choose_kernel, "choose", shapes, pos, *operands)


def pair_kernel(pos, own_ref, got_ref, pair_ref):
    even = is_even(pos)
    pair_ref[:STATE] = jnp.where(even, own_ref[...], got_ref[...])
    pair_ref[STATE:] = jnp.where(even, got_ref[...], own_ref[...])


def make_pair(pos, own, got):
    return small(pair_kernel, "make_pair", ((PAIR, TILE),), pos, own, got)[0]


def last_step_kernel(pos, one_ref, seven_ref, three_ref, five_ref, up_ref, down_ref):
    rows = one_ref.shape[0]
    cut = half(rows)
    up_ref[:rows] = seven_ref[...]
    up_ref[rows:] = five_ref[:cut]
    down_ref[:rows] = one_ref[...]
    down_ref[rows:] = three_ref[cut:]


def last_step(pos, one, seven, three, five):
    rows = one.shape[0]
    cut = half(rows)
    shapes = ((rows + cut, TILE), (2 * rows - cut, TILE))
    return small(last_step_kernel, "last_step", shapes, pos, one, seven, three, five)


def prepare_kernel(b_ref, c_ref, scores, scores_t, b_turned, c_turned):
    square = (TILE, TILE)
    upper = iota(square, 0) <= iota(square, 1)
    lower = iota(square, 0) >= iota(square, 1)
    for block in range(scores.shape[0]):
        at = slice(block * TILE, (block + 1) * TILE)
        b_rows, c_rows = b_ref[at, :], c_ref[at, :]
        scores[block] = jnp.where(lower, dot(c_rows, b_rows, ((1,), (1,))), 0.0)
        scores_t[block] = jnp.where(upper, dot(b_rows, c_rows, ((1,), (1,))), 0.0)
        b_turned[:, at] = b_rows.astype(F32).T.astype(BF16)
        c_turned[:, at] = c_rows.astype(F32).T.astype(BF16)


def prepare(b, c):
    tokens, state = b.shape
    square = jax.ShapeDtypeStruct((tokens // TILE, TILE, TILE), F32)
    turned = jax.ShapeDtypeStruct((state, tokens), BF16)
    return pl.pallas_call(
        prepare_kernel,
        out_shape=(square, square, turned, turned),
        in_specs=[VMEM, VMEM],
        out_specs=(VMEM,) * 4,
        compiler_params=params(),
        cost_estimate=pl.CostEstimate(flops=10**8, bytes_accessed=2 << 20, transcendentals=0),
        name="prepare",
    )(b, c)


def mix_kernel(
    group, pos, x_ref, dy_ref, b_ref, c_ref, cols_ref, rows_ref,
    scores, scores_t, b_turned, c_turned, *rest
):
    (
        y_hbm, dx_hbm, y_ref, dx_ref, inner_dx, out_scale, wdy, state, ends, left,
    ) = rest[-10:]
    length = pos[2]
    tokens, width = y_ref.shape
    blocks = tokens // TILE
    square = (TILE, TILE)
    ours = pl.ds(group * width, width)

    low = iota(square, 1) < HALF

    def split(value):
        return jnp.concatenate(
            [jnp.where(low, value, 0.0), jnp.where(low, 0.0, value)], 0
        ).astype(BF16)

    state[...] = jnp.zeros_like(state)

    for block in range(blocks):
        at = slice(block * TILE, (block + 1) * TILE)
        cols = pltpu.roll(cols_ref[at, :], (TILE - 4 * group) % TILE, 1)
        live = iota(square, 0) + block * TILE < length
        rows = rows_ref[group // 2 * 8 : group // 2 * 8 + 8, at]
        rows = rows[4 * (group % 2) : 4 * (group % 2) + 4]
        held = state[...]
        carried = dot(c_ref[at, :], held.astype(BF16))
        update, end = [], []
        for part in range(2):
            lanes = slice(part * TILE, (part + 1) * TILE)
            tile = slice(group * width + part * TILE, group * width + (part + 1) * TILE)
            x = x_ref[at, tile].astype(F32)
            dy = jnp.where(live, dy_ref[at, tile].astype(F32), 0.0)
            gain = spread(cols[:8], 96 + 2 * part, low[:8])[:1]
            sides = [
                jnp.broadcast_to(cols[:, 2 * part + k : 2 * part + k + 1], square)
                for k in range(2)
            ]
            step = spread(cols, 32 + 2 * part, low)
            log = jnp.where(low, sides[0], sides[1])
            last = log[TILE - 1 :]
            since = jnp.exp2(log)
            until = jnp.exp2(last - log)
            ahead, back = [], []
            for k in range(2):
                gap = sides[k] - rows[2 * part + k : 2 * part + k + 1]
                ahead.append((jnp.exp2(jnp.minimum(gap, 0.0)) * scores[block]).astype(BF16))
                back.append((jnp.exp2(jnp.minimum(-gap, 0.0)) * scores_t[block]).astype(BF16))
            stepped = x * step
            y = dot(jnp.concatenate(ahead, 1), split(stepped)) + gain * x
            y = y + since * carried[:, lanes]
            y_ref[at, lanes] = jnp.where(live, y, 0.0)
            dx = dot(jnp.concatenate(back, 1), split(dy))
            inner_dx[at, lanes] = step * dx + gain * dy
            out_scale[at, lanes] = step * until
            wdy[at, lanes] = (dy * since).astype(BF16)
            update.append((stepped * until).astype(BF16))
            end.append(jnp.exp2(last))
        end = jnp.concatenate(end, 1)
        ends[block] = jnp.broadcast_to(end, ends.shape[1:])
        state[...] = end * held + dot(b_turned[:, at], jnp.concatenate(update, 1))

    out_y = pltpu.make_async_copy(y_ref, y_hbm.at[group], left.at[0])
    out_y.start()
    state[...] = jnp.zeros_like(state)

    for block in reversed(range(blocks)):
        at = slice(block * TILE, (block + 1) * TILE)
        held = state[...]
        dx = inner_dx[at, :] + out_scale[at, :] * dot(b_ref[at, :], held.astype(BF16))
        dx_ref[at, :] = dx.astype(BF16)
        state[...] = ends[block][:1] * held + dot(c_turned[:, at], wdy[at, :])

    out_dx = pltpu.make_async_copy(dx_ref, dx_hbm.at[:, ours], left.at[1])
    out_dx.start()
    out_y.wait()
    out_dx.wait()


def mix(group, pos, x, dy, b, c, cols, rows, prepared, before):
    tokens, total = x.shape
    state = b.shape[1]
    width = total // RING
    blocks = tokens // TILE
    operands = [pos, x, dy, b, c, cols, rows, *prepared]
    specs = [SMEM] + [VMEM] * (len(operands) - 1)
    alias = {}
    if before is not None:
        alias = {len(operands): 0, len(operands) + 1: 1}
        specs += [HBM, HBM]
        operands += list(before)
    return pl.pallas_call(
        functools.partial(mix_kernel, group),
        out_shape=(
            jax.ShapeDtypeStruct((RING, tokens, width), F32),
            jax.ShapeDtypeStruct((tokens, total), BF16),
        ),
        in_specs=specs,
        out_specs=(HBM, HBM),
        scratch_shapes=[
            pltpu.VMEM((tokens, width), F32),
            pltpu.VMEM((tokens, width), BF16),
            pltpu.VMEM((tokens, width), F32),
            pltpu.VMEM((tokens, width), F32),
            pltpu.VMEM((tokens, width), BF16),
            pltpu.VMEM((state, width), F32),
            pltpu.VMEM((blocks, 8, width), F32),
            pltpu.SemaphoreType.DMA((2,)),
        ],
        input_output_aliases=alias,
        compiler_params=params(),
        cost_estimate=pl.CostEstimate(
            flops=8 * tokens * width * state, bytes_accessed=4 << 20, transcendentals=0
        ),
        name="mix",
    )(*operands)


def finish_kernel(
    pos, c_ref, entries_ref, y_hbm, p0, p1, p7, p3, p5, up_ref, down_ref, out_hbm,
    state, y_all, out_all, arrived, left,
):
    tokens, width = out_all.shape[1:]

    def store(place):
        start = pl.multiple_of(lax.rem(place + along(pos), RING) * width, width)
        target = out_hbm.at[:, pl.ds(start, width)]
        return pltpu.make_async_copy(out_all.at[place], target, left.at[place])

    def load(place):
        source = y_hbm.at[lax.rem(place + along(pos), RING)]
        return pltpu.make_async_copy(source, y_all.at[place], arrived.at[place])

    for place in range(RING):
        load(place).start()

    tiles = [(ref.at[:STATE], ref.at[STATE:PAIR]) for ref in (p0, p1, down_ref, p3)]
    tiles.append((up_ref.at[PAIR:], down_ref.at[PAIR:]))
    tiles += [(ref.at[:STATE], ref.at[STATE:PAIR]) for ref in (p5, up_ref, p7)]
    for place, (first, second) in enumerate(tiles):
        state[place, :, :TILE] = first[...].astype(BF16)
        state[place, :, TILE:] = second[...].astype(BF16)

    def group_of_heads(ahead, carry):
        group = lax.rem(ahead + along(pos), RING)
        scale = scale_of(group, entries_ref, width)
        carried = scale * dot(c_ref[...], state[ahead])
        load(ahead).wait()
        y = y_all[ahead] + carried
        out_all[ahead] = y.astype(BF16)
        store(ahead).start()
        return carry

    lax.fori_loop(0, RING, group_of_heads, 0)
    for place in range(RING):
        store(place).wait()


def finish(pos, c, entries, y, pairs):
    _, tokens, width = y.shape
    return pl.pallas_call(
        finish_kernel,
        in_specs=[SMEM, VMEM, VMEM, HBM] + [VMEM] * len(pairs),
        out_specs=HBM,
        scratch_shapes=[
            pltpu.VMEM((RING, 2 * TILE, width), BF16),
            pltpu.VMEM((RING, tokens, width), F32),
            pltpu.VMEM((RING, tokens, width), BF16),
            pltpu.SemaphoreType.DMA((RING,)),
            pltpu.SemaphoreType.DMA((RING,)),
        ],
        out_shape=jax.ShapeDtypeStruct((tokens, RING * width), BF16),
        compiler_params=params(58),
        cost_estimate=pl.CostEstimate(
            flops=2 * tokens * width * RING * 256, bytes_accessed=10 << 20, transcendentals=0
        ),
        name="finish",
    )(pos, c, entries, y, *pairs)


def back_kernel(
    pos, b_ref, got_ref, p0, p1, p7, p3, p5, up_ref, down_ref, own_ref, send_ref
):
    mine = b_ref[...]
    other = jnp.concatenate([got_ref[RING], got_ref[RING + 1]], 1).astype(BF16)
    opposite = jnp.concatenate([up_ref[FULL:], down_ref[FULL:]], 0)
    for place, ref in enumerate((p0, p1, down_ref, p3, opposite, p5, up_ref, p7)):
        grad = ref[:STATE].astype(BF16)
        own_ref[place] = dot(mine, grad)
        send_ref[place, :TILE] = dot(other, grad)
        send_ref[place, TILE:] = ref[STATE:FULL]


def back(pos, *operands):
    shapes = ((RING, TILE, TILE), (RING, TILE + 8, TILE))
    return small(back_kernel, "back", shapes, pos, *operands, nbytes=4 << 20)


def prompt_dx_kernel(
    pos, own_ref, sent_ref, got_ref, cols_ref, fade_ref, out_hbm, skip_ref, out_all, left
):
    even = is_even(pos)
    low = iota((TILE, TILE), 1) < HALF
    scale = cols_ref[...] * pltpu.roll(fade_ref[...], TILE - 32, 1)[:1]
    width = out_all.shape[2]

    def store(place):
        start = pl.multiple_of(lax.rem(place + along(pos), RING) * width, width)
        target = out_hbm.at[:, pl.ds(start, width)]
        return pltpu.make_async_copy(out_all.at[place], target, left.at[place])

    def group_of_heads(ahead, carry):
        group = lax.rem(ahead + along(pos), RING)
        cols = pltpu.roll(scale, lax.rem(TILE - 4 * group, TILE), 1)
        own, got = own_ref[ahead], got_ref[ahead, :TILE]
        tiles = (jnp.where(even, own, got), jnp.where(even, got, own))
        for part in range(2):
            lanes = slice(part * TILE, (part + 1) * TILE)
            out_all[ahead, :, lanes] = (tiles[part] * spread(cols, 2 * part, low)).astype(BF16)
        store(ahead).start()
        own, got = sent_ref[ahead, TILE : TILE + 8], got_ref[ahead, TILE : TILE + 8]
        skip_ref[group, 0] = jnp.where(even, own, got)
        skip_ref[group, 1] = jnp.where(even, got, own)
        return carry

    lax.fori_loop(0, RING, group_of_heads, 0)
    for place in range(RING):
        store(place).wait()


def prompt_gradient(pos, own, sent, got, cols, fade):
    return pl.pallas_call(
        prompt_dx_kernel,
        in_specs=[SMEM] + [VMEM] * 5,
        out_specs=(HBM, VMEM),
        scratch_shapes=[
            pltpu.VMEM((RING, TILE, 2 * TILE), BF16),
            pltpu.SemaphoreType.DMA((RING,)),
        ],
        out_shape=(
            jax.ShapeDtypeStruct((TILE, RING * 2 * TILE), BF16),
            jax.ShapeDtypeStruct((RING, 2, 8, TILE), F32),
        ),
        compiler_params=params(),
        cost_estimate=pl.CostEstimate(flops=10**6, bytes_accessed=2 << 20, transcendentals=0),
        name="prompt_gradient",
    )(pos, own, sent, got, cols, fade)


def along_z(value, distance):
    pairs = [
        (2 * z + y, 2 * ((z + distance) % RING) + y) for z in range(RING) for y in range(2)
    ]
    return lax.ppermute(value, "sample", pairs)


def swap(value, bit=1):
    return lax.ppermute(value, "sample", [(s, s ^ bit) for s in range(2 * RING)])


def along_dp(value, distance):
    return lax.ppermute(value, "dp", [(i, (i + distance) % 4) for i in range(4)])


def together(*values):
    return lax.optimization_barrier(values)


def body(
    prompt_x, prompt_b, prompt_step, resp_x, resp_b, resp_c, resp_step,
    decay_rate, skip_gain, lengths, prompt_map, resp_cotangent,
):
    place = lax.axis_index("sample")
    here = lax.axis_index("dp")
    pos = jnp.concatenate(
        [place[None].astype(jnp.int32), here[None].astype(jnp.int32), lengths[0], prompt_map]
    )
    rate, gain = decay_rate[None], skip_gain[None]
    x, dy, b, c = resp_x[0, 0], resp_cotangent[0, 0], resp_b[0, 0], resp_c[0, 0]

    mine = sum_logs(prompt_step[0], rate)
    other = swap(mine)
    gain, _ = together(gain, mine)
    sent, own, coef, down, up, cols, rows, turned, entries = begin(
        pos, prompt_step[0], rate, gain, prompt_b[0], prompt_x[0], resp_step[0, 0], c, dy
    )
    other, sent = together(other, sent)
    got = swap(sent)
    down, up = along_z(down, -1), along_z(up, 1)

    after_own = jnp.where(place & 1 == 0, other, 0.0)
    after_got = jnp.where(place & 1 == 0, 0.0, mine)

    def add_later(after_own, after_got, total, other, bit):
        later = jnp.where(place & bit == 0, other, 0.0)
        return after_own + later, after_got + later, total + other

    total = mine + other
    other = swap(total, 2)
    entries, _ = together(entries, total)
    rest, gains, kept = other_grads(pos, dy, x, turned, entries)
    after_own, after_got, total = add_later(after_own, after_got, total, other, 2)
    rest, total = together(rest, total)
    other = swap(total, 4)

    b_ready, _ = together(b, rest)
    prepared = prepare(b_ready, c)
    groups = iter(range(RING))

    def within(before, after, count=2):
        for _ in range(count):
            ready, _ = together(x, after)
            before = mix(next(groups), pos, ready, dy, b, c, cols, rows, prepared, before)
        return before

    five, three = pass_first(pos, rest, down, up)
    after_own, after_got, total = add_later(after_own, after_got, total, other, 4)
    gains, five, three, total = together(gains, five, three, total)
    other = swap(total, 8)
    came = swap(gains)
    five, three = along_z(five, -2), along_z(three, 2)
    after_own, after_got, total = add_later(after_own, after_got, total, other, 8)

    down_a, up_a, rest_a, fade = contributions(
        pos, own, got, prompt_b[0], after_own, after_got, kept, came
    )
    down_a, up_a = along_z(down_a, -1), along_z(up_a, 1)
    mixed = within(None, rest_a, 1)
    rest, rest_a, mixed = together(rest, rest_a, mixed)

    seven, one = pass_second(pos, rest, down, up, five, three)
    five, three = pass_first(pos, rest_a, down_a, up_a)
    seven, one, five, three = together(seven, one, five, three)
    seven, one = along_z(seven, -1), along_z(one, 1)
    five, three = along_z(five, -2), along_z(three, 2)
    mixed = within(mixed, fade)
    rest, rest_a, mixed = together(rest, rest_a, mixed)

    grad_own, grad_send = own_tile(pos, rest, seven, one)
    seven, one = pass_second(pos, rest_a, down_a, up_a, five, three)
    grad_send, seven, one = together(grad_send, seven, one)
    grad_got = swap(grad_send)
    seven, one = along_z(seven, -1), along_z(one, 1)
    mixed = within(mixed, grad_own, 1)
    rest_a, mixed = together(rest_a, mixed)
    share = make_share(pos, rest_a, seven, one, grad_own, grad_got)

    others = [along_dp(share, d) for d in (1, 2, 3)]
    mixed = within(mixed, share)
    share, mixed = together(share, mixed)
    message, start = choose(pos, share, *others)

    start_got = swap(start)
    one, seven = along_z(message, -1), along_z(message, 1)
    one, seven, start_got = together(one, seven, start_got)
    pair = make_pair(pos, start, start_got)
    three, five = along_z(one, -2), along_z(seven, 2)
    pair_one, pair_seven = along_z(pair, -1), along_z(pair, 1)
    mixed = within(mixed, pair, 1)
    three, five, pair_one, pair_seven, mixed = together(
        three, five, pair_one, pair_seven, mixed
    )
    up, down = last_step(pos, one, seven, three, five)
    up, down = along_z(up, 1), along_z(down, -1)
    pair_three, pair_five = along_z(pair_one, -2), along_z(pair_seven, 2)
    mixed = within(mixed, pair_one, 1)
    up, down, pair_three, pair_five, mixed = together(up, down, pair_three, pair_five, mixed)
    own_dx, sent = back(pos, prompt_b[0], got, message, one, seven, three, five, up, down)
    got_last = swap(sent)
    pair_one, _ = together(pair_one, sent)
    pair_up, pair_down = last_step(pos, pair_one, pair_seven, pair_three, pair_five)
    pair_up, pair_down = along_z(pair_up, 1), along_z(pair_down, -1)
    prompt_dx, skip = prompt_gradient(pos, own_dx, sent, got_last, coef, fade)
    skip_grad = jnp.sum(skip[:, :, 0].reshape(-1, HALF), 1)
    pair_up, pair_down, skip_grad = together(pair_up, pair_down, skip_grad)
    pairs = [pair, pair_one, pair_seven, pair_three, pair_five, pair_up, pair_down]
    resp_y = finish(pos, c, entries, mixed[0], pairs)
    return (resp_y[None, None], mixed[1][None, None], prompt_dx[None], skip_grad)


def solution(mesh):
    placed = (
        P("dp", "sample", "tensor"),
        P("dp", "sample", None),
        P("dp", "tensor", "sample"),
        P("dp", "sample", None, "tensor"),
        P("dp", "sample", None, None),
        P("dp", "sample", None, None),
        P("dp", "sample", "tensor", None),
        P("tensor"),
        P("tensor"),
        P("dp", "sample"),
        P(),
        P("dp", "sample", None, "tensor"),
    )
    return jax.shard_map(
        body,
        mesh=mesh,
        in_specs=placed,
        out_specs=(
            P("dp", "sample", None, "tensor"),
            P("dp", "sample", None, "tensor"),
            P("dp", "sample", "tensor"),
            P("tensor"),
        ),
        check_vma=False,
    )
```

```python
import functools

import jax
import jax.numpy as jnp
from jax import lax
from jax.experimental import pallas as pl
from jax.experimental.pallas import tpu as pltpu
from jax.sharding import PartitionSpec as P

F32 = jnp.float32
BF16 = jnp.bfloat16
LOG2E = 1.4426950408889634
EXACT = lax.Precision.HIGHEST
TILE = 128
HALF = 64
RING = 8
STATE = 2 * TILE
PAIR = 2 * STATE
FULL = STATE + 8
KEPT = (0, 1, 3, 5, 7)
VMEM = pl.BlockSpec(memory_space=pltpu.VMEM)
SMEM = pl.BlockSpec(memory_space=pltpu.SMEM)
HBM = pl.BlockSpec(memory_space=pltpu.HBM)


def dot(left, right, dims=((1,), (0,)), precision=None):
    return lax.dot_general(
        left, right, (dims, ((), ())), precision=precision, preferred_element_type=F32
    )


def iota(shape, axis):
    return lax.broadcasted_iota(jnp.int32, shape, axis)


def along(pos):
    return lax.axis_index("sample") >> 1


def is_even(pos):
    return lax.axis_index("sample") & 1 == 0


def column(row):
    heads = row.shape[1]
    square = (heads, heads)
    return jnp.sum(jnp.where(iota(square, 0) == iota(square, 1), row, 0.0), 1, keepdims=True)


def params(megabytes=14):
    return pltpu.CompilerParams(vmem_limit_bytes=megabytes << 20)


def spread(cols, first, low):
    return jnp.where(low, cols[:, first : first + 1], cols[:, first + 1 : first + 2])


def sum_logs_kernel(step_ref, rate_ref, out_ref):
    log = -(step_ref[...] * column(rate_ref[...]))
    heads = log.shape[0]
    total = dot(jnp.ones((8, TILE), F32), log, ((1,), (1,)), EXACT)
    blank = jnp.zeros((8, TILE - 2 * heads), F32)
    out_ref[...] = jnp.concatenate([jnp.zeros((8, heads), F32), total, blank], 1)


def sum_logs(step, rate):
    return pl.pallas_call(
        sum_logs_kernel,
        out_shape=jax.ShapeDtypeStruct((8, TILE), F32),
        in_specs=[VMEM, VMEM],
        out_specs=VMEM,
        compiler_params=params(61),
        cost_estimate=pl.CostEstimate(flops=10**5, bytes_accessed=1 << 15, transcendentals=0),
        name="sum_logs",
    )(step, rate)


def scale_of(group, entries_ref, width):
    head = 4 * group + iota((TILE, width), 1) // HALF
    row = iota((TILE, width), 0)
    chosen = (row < 64) & (row % 32 == head)
    return dot(entries_ref[...], chosen.astype(F32).astype(BF16))


def weigh_group(group, dy, entries_ref, weighted):
    scale = scale_of(group, entries_ref, weighted.shape[1])
    weighted[...] = (dy.astype(F32) * scale).astype(BF16)


FIRST = (6, 2, 4)


def begin_kernel(
    pos, *refs
):
    sources, rest = refs[:8], refs[8:]
    (sent_ref, own_ref, coef_ref, down_ref, up_ref, cols_ref, rows_ref, turned,
     entries_ref) = rest[:9]
    targets, (dy_ref, weighted, arrived) = rest[9:16], rest[16:]
    even = is_even(pos)
    length = pos[0]
    tokens, width = weighted.shape
    groups = [lax.rem(place + along(pos), RING) for place in FIRST]
    copies = [
        pltpu.make_async_copy(source, target, arrived.at[index])
        for index, (source, target) in enumerate(zip(sources, targets))
    ]
    for index, group in enumerate(groups):
        at = pl.ds(pl.multiple_of(group * width, width), width)
        copies.append(
            pltpu.make_async_copy(sources[7].at[:, at], dy_ref.at[index], arrived.at[7 + index])
        )
    for copy in copies:
        copy.start()
    for copy in copies[:5]:
        copy.wait()
    ps_ref, rate_ref, gain_ref, pb_ref, px_ref, step_ref, c_ref = targets

    square = (TILE, TILE)
    rate = column(rate_ref[...])
    step = ps_ref[...]
    heads = step.shape[0]
    log = -(step * rate)
    later = (iota(square, 0) > iota(square, 1)).astype(F32)
    coef = jnp.exp(dot(log, later, precision=EXACT)) * step
    cols = jnp.concatenate([coef, jnp.zeros((TILE - heads, TILE), F32)], 0).T
    coef_ref[...] = cols
    low = iota(square, 1) < HALF
    for place in range(RING):
        pair = []
        for part in range(2):
            tile = 2 * place + part
            x = px_ref[:, tile * TILE : (tile + 1) * TILE].astype(F32)
            pair.append(x * spread(cols, 2 * tile, low))
        own_ref[place] = jnp.where(even, pair[0], pair[1]).astype(BF16)
        sent_ref[place] = jnp.where(even, pair[1], pair[0]).astype(BF16).astype(F32)
    sent_ref[RING] = pb_ref[:, :TILE].astype(F32)
    sent_ref[RING + 1] = pb_ref[:, TILE:].astype(F32)

    copies[5].wait()
    copies[6].wait()
    step = step_ref[...]
    log = step * rate * (-LOG2E)
    gain = jnp.broadcast_to(column(gain_ref[...]), (heads, TILE))
    upto = (iota(square, 0) <= iota(square, 1)).astype(F32)
    run = jnp.zeros((heads, 1), F32)
    blank = jnp.zeros((TILE - 2 * heads, TILE), F32)
    for block in range(tokens // TILE):
        at = slice(block * TILE, (block + 1) * TILE)
        turned[:, at] = c_ref[at, :].astype(F32).T.astype(BF16)
        cum = dot(log[:, at], upto, precision=EXACT)
        rows_ref[:, at] = cum
        whole = cum + run
        run = whole[:, TILE - 1 :]
        live = iota((heads, TILE), 1) + block * TILE < length
        entry = jnp.where(live, jnp.exp2(whole), 0.0)
        cols_ref[at, :] = jnp.concatenate([cum, step[:, at], entry, gain], 0).T
        high = entry.astype(BF16).astype(F32)
        entries_ref[at, :] = jnp.concatenate([high, entry - high, blank], 0).T.astype(BF16)

    for index, group in enumerate(groups):
        copies[7 + index].wait()
        weigh_group(group, dy_ref[index], entries_ref, weighted)
        grad = dot(turned[...], weighted[...])
        if FIRST[index] == 4:
            down_ref[PAIR:] = grad[:, :TILE]
            up_ref[PAIR:] = grad[:, TILE:]
        else:
            ref = down_ref if FIRST[index] == 6 else up_ref
            ref[:STATE] = grad[:, :TILE]
            ref[STATE:PAIR] = grad[:, TILE:]


def begin(pos, ps, rate, gain, pb, px, step, c, dy):
    tokens, width = dy.shape
    state = c.shape[1]
    heads = step.shape[0]
    shape = jax.ShapeDtypeStruct
    small_ones = (ps, rate, gain, pb, px, step, c)
    return pl.pallas_call(
        begin_kernel,
        in_specs=[SMEM] + [HBM] * 8,
        out_specs=(VMEM,) * 9,
        scratch_shapes=[pltpu.VMEM(operand.shape, operand.dtype) for operand in small_ones]
        + [
            pltpu.VMEM((len(FIRST), tokens, width // RING), BF16),
            pltpu.VMEM((tokens, width // RING), BF16),
            pltpu.SemaphoreType.DMA((7 + len(FIRST),)),
        ],
        out_shape=(
            shape((RING + 2, TILE, TILE), F32), shape((RING, TILE, TILE), BF16),
            shape((TILE, TILE), F32),
            shape((PAIR + STATE, TILE), F32), shape((PAIR + STATE, TILE), F32),
            shape((tokens, TILE), F32), shape((heads, tokens), F32),
            shape((state, tokens), BF16), shape((tokens, TILE), BF16),
        ),
        compiler_params=params(60),
        cost_estimate=pl.CostEstimate(
            flops=tokens * width * state, bytes_accessed=4 << 20, transcendentals=0
        ),
        name="begin",
    )(pos, *small_ones, dy)


def other_grads_kernel(
    pos, dy_ref, x_ref, turned, entries_ref, rest_ref, send_ref, keep_ref, weighted
):
    even = is_even(pos)
    length = pos[0]
    tokens, width = weighted.shape

    def piece(slot, carry):
        ahead = jnp.where(slot < 1, 0, 2 * slot - 1)
        group = lax.rem(ahead + along(pos), RING)
        at = pl.ds(pl.multiple_of(group * width, width), width)
        weigh_group(group, dy_ref[:, at], entries_ref, weighted)
        grad = dot(turned[...], weighted[...])
        rest_ref[slot, :STATE] = grad[:, :TILE]
        rest_ref[slot, STATE:] = grad[:, TILE:]
        return carry

    def gain_of_group(ahead, carry):
        group = lax.rem(ahead + along(pos), RING)
        gains = [jnp.zeros((1, TILE), F32)] * 2
        for block in range(tokens // TILE):
            at = slice(block * TILE, (block + 1) * TILE)
            live = iota((TILE, TILE), 0) + block * TILE < length
            for part in range(2):
                tile = pl.ds(pl.multiple_of((2 * group + part) * TILE, TILE), TILE)
                product = dy_ref[at, tile].astype(F32) * x_ref[at, tile].astype(F32)
                product = jnp.where(live, product, 0.0)
                gains[part] = gains[part] + jnp.sum(product, 0, keepdims=True)
        gains = [jnp.broadcast_to(gain, (8, TILE)) for gain in gains]
        keep_ref[ahead] = jnp.where(even, gains[0], gains[1])
        send_ref[ahead] = jnp.where(even, gains[1], gains[0])
        return carry

    lax.fori_loop(0, len(KEPT), piece, 0)
    lax.fori_loop(0, RING, gain_of_group, 0)


def other_grads(pos, dy, x, turned, entries):
    tokens, width = dy.shape
    shapes = ((len(KEPT), PAIR, TILE), (RING, 8, TILE), (RING, 8, TILE))
    return pl.pallas_call(
        other_grads_kernel,
        in_specs=[SMEM] + [VMEM] * 4,
        out_specs=(VMEM,) * len(shapes),
        scratch_shapes=[pltpu.VMEM((tokens, width // RING), BF16)],
        out_shape=tuple(jax.ShapeDtypeStruct(shape, F32) for shape in shapes),
        compiler_params=params(),
        cost_estimate=pl.CostEstimate(
            flops=2 * tokens * width * 256, bytes_accessed=8 << 20, transcendentals=0
        ),
        name="other_grads",
    )(pos, dy, x, turned, entries)


def small(kernel, name, shapes, pos, *operands, nbytes=2 << 20):
    return pl.pallas_call(
        kernel,
        out_shape=tuple(jax.ShapeDtypeStruct(shape, F32) for shape in shapes),
        in_specs=[SMEM] + [VMEM] * len(operands),
        out_specs=(VMEM,) * len(shapes),
        compiler_params=params(),
        cost_estimate=pl.CostEstimate(flops=10**6, bytes_accessed=nbytes, transcendentals=0),
        name=name,
    )(pos, *operands)


def half(rows):
    return rows // 16 * 8 + rows % 16


def pass_first_kernel(pos, rest_ref, down_ref, up_ref, five_ref, three_ref):
    rows = five_ref.shape[0]
    cut = half(rows)
    five_ref[:cut] = rest_ref[3, :cut] + down_ref[rows:]
    five_ref[cut:] = rest_ref[3, cut:]
    three_ref[:cut] = rest_ref[2, :cut]
    three_ref[cut:] = rest_ref[2, cut:] + up_ref[rows:]


def pass_first(pos, rest, down, up):
    return small(pass_first_kernel, "pass_first", (rest.shape[1:],) * 2, pos, rest, down, up)


def pass_second_kernel(
    pos, rest_ref, down_ref, up_ref, far_down_ref, far_up_ref, seven_ref, one_ref
):
    rows = seven_ref.shape[0]
    seven_ref[...] = rest_ref[4] + down_ref[:rows] + far_down_ref[...]
    one_ref[...] = rest_ref[1] + up_ref[:rows] + far_up_ref[...]


def pass_second(pos, rest, *operands):
    shapes = (rest.shape[1:],) * 2
    return small(pass_second_kernel, "pass_second", shapes, pos, rest, *operands)


def own_tile_kernel(pos, rest_ref, down_ref, up_ref, own_ref, send_ref):
    even = is_even(pos)
    first, second = slice(0, STATE), slice(STATE, PAIR)
    first = rest_ref[0, first] + down_ref[first] + up_ref[first]
    second = rest_ref[0, second] + down_ref[second] + up_ref[second]
    own_ref[...] = jnp.where(even, first, second)
    send_ref[...] = jnp.where(even, second, first)


def own_tile(pos, *operands):
    return small(own_tile_kernel, "own_tile", ((STATE, TILE),) * 2, pos, *operands)


def contrib_kernel(
    pos, own_ref, got_ref, b_ref, after_ref, after_got_ref, keep_ref, came_ref,
    down_ref, up_ref, rest_ref, fade_ref,
):
    turned = b_ref[...].astype(F32).T.astype(BF16)
    turned_got = jnp.concatenate([got_ref[RING].T, got_ref[RING + 1].T], 0).astype(BF16)
    low = iota((8, TILE), 1) < HALF
    fades = (jnp.exp(after_ref[...]), jnp.exp(after_got_ref[...]))
    fade_ref[...] = fades[0]
    cut = half(FULL)
    for ahead in range(RING):
        place = lax.rem(along(pos) + ahead, RING)
        shift = lax.rem(2 * TILE - 32 - 4 * place - 2 * (lax.axis_index("sample") & 1), TILE)
        scales = [spread(pltpu.roll(fade, shift, 1), 0, low)[:1] for fade in fades]
        own = dot(turned, own_ref[place])
        got = dot(turned_got, got_ref[place].astype(BF16))
        piece = jnp.concatenate(
            [own * scales[0] + got * scales[1], keep_ref[ahead] + came_ref[ahead]], 0
        )
        if ahead == 4:
            down_ref[FULL:] = piece[:cut]
            up_ref[FULL:] = piece[cut:]
        elif ahead in KEPT:
            rest_ref[KEPT.index(ahead)] = piece
        else:
            ref = down_ref if ahead == 6 else up_ref
            ref[:FULL] = piece


def contributions(pos, *operands):
    cut = half(FULL)
    shapes = (
        (FULL + cut, TILE), (2 * FULL - cut, TILE), (len(KEPT), FULL, TILE), (8, TILE),
    )
    return small(contrib_kernel, "contributions", shapes, pos, *operands, nbytes=6 << 20)


def share_kernel(pos, rest_ref, down_ref, up_ref, own_ref, got_ref, share_ref):
    share_ref[:FULL] = rest_ref[0] + down_ref[...] + up_ref[...]
    share_ref[FULL:] = own_ref[...] + got_ref[...]


def make_share(pos, *operands):
    return small(share_kernel, "make_share", ((FULL + STATE, TILE),), pos, *operands)[0]


def choose_kernel(pos, first, second, third, fourth, message_ref, start_ref):
    here = lax.axis_index("dp")
    distance_to_start = (here - pos[here]) & 3
    shares = (first, second, third, fourth)
    start = first[:STATE]
    grad = jnp.zeros((STATE, TILE), F32)
    gains = jnp.zeros((8, TILE), F32)
    for distance, ref in enumerate(shares):
        start = jnp.where(distance_to_start == distance, ref[:STATE], start)
        mine = pos[(here - distance) & 3] == here
        grad = grad + jnp.where(mine, ref[FULL:], 0.0)
        gains = gains + ref[STATE:FULL]
    message_ref[:STATE] = grad
    message_ref[STATE:] = gains
    start_ref[...] = start


def choose(pos, *operands):
    shapes = ((FULL, TILE), (STATE, TILE))
    return small(choose_kernel, "choose", shapes, pos, *operands)


def pair_kernel(pos, own_ref, got_ref, pair_ref):
    even = is_even(pos)
    pair_ref[:STATE] = jnp.where(even, own_ref[...], got_ref[...])
    pair_ref[STATE:] = jnp.where(even, got_ref[...], own_ref[...])


def make_pair(pos, own, got):
    return small(pair_kernel, "make_pair", ((PAIR, TILE),), pos, own, got)[0]


def last_step_kernel(pos, one_ref, seven_ref, three_ref, five_ref, up_ref, down_ref):
    rows = one_ref.shape[0]
    cut = half(rows)
    up_ref[:rows] = seven_ref[...]
    up_ref[rows:] = five_ref[:cut]
    down_ref[:rows] = one_ref[...]
    down_ref[rows:] = three_ref[cut:]


def last_step(pos, one, seven, three, five):
    rows = one.shape[0]
    cut = half(rows)
    shapes = ((rows + cut, TILE), (2 * rows - cut, TILE))
    return small(last_step_kernel, "last_step", shapes, pos, one, seven, three, five)


def prepare_kernel(b_ref, c_ref, scores, scores_t, b_turned, c_turned):
    square = (TILE, TILE)
    upper = iota(square, 0) <= iota(square, 1)
    lower = iota(square, 0) >= iota(square, 1)
    for block in range(scores.shape[0]):
        at = slice(block * TILE, (block + 1) * TILE)
        b_rows, c_rows = b_ref[at, :], c_ref[at, :]
        scores[block] = jnp.where(lower, dot(c_rows, b_rows, ((1,), (1,))), 0.0)
        scores_t[block] = jnp.where(upper, dot(b_rows, c_rows, ((1,), (1,))), 0.0)
        b_turned[:, at] = b_rows.astype(F32).T.astype(BF16)
        c_turned[:, at] = c_rows.astype(F32).T.astype(BF16)


def prepare(b, c):
    tokens, state = b.shape
    square = jax.ShapeDtypeStruct((tokens // TILE, TILE, TILE), F32)
    turned = jax.ShapeDtypeStruct((state, tokens), BF16)
    return pl.pallas_call(
        prepare_kernel,
        out_shape=(square, square, turned, turned),
        in_specs=[VMEM, VMEM],
        out_specs=(VMEM,) * 4,
        compiler_params=params(),
        cost_estimate=pl.CostEstimate(flops=10**8, bytes_accessed=2 << 20, transcendentals=0),
        name="prepare",
    )(b, c)


def mix_kernel(
    group, pos, x_ref, dy_ref, b_ref, c_ref, cols_ref, rows_ref,
    scores, scores_t, b_turned, c_turned, *rest
):
    (
        y_hbm, dx_hbm, y_ref, dx_ref, inner_dx, out_scale, wdy, state, ends, left,
    ) = rest[-10:]
    length = pos[0]
    tokens, width = y_ref.shape
    blocks = tokens // TILE
    square = (TILE, TILE)
    ours = pl.ds(group * width, width)

    low = iota(square, 1) < HALF

    def split(value):
        return jnp.concatenate(
            [jnp.where(low, value, 0.0), jnp.where(low, 0.0, value)], 0
        ).astype(BF16)

    state[...] = jnp.zeros_like(state)

    for block in range(blocks):
        at = slice(block * TILE, (block + 1) * TILE)
        cols = pltpu.roll(cols_ref[at, :], (TILE - 4 * group) % TILE, 1)
        live = iota(square, 0) + block * TILE < length
        rows = rows_ref[group // 2 * 8 : group // 2 * 8 + 8, at]
        rows = rows[4 * (group % 2) : 4 * (group % 2) + 4]
        held = state[...]
        carried = dot(c_ref[at, :], held.astype(BF16))
        update, end = [], []
        for part in range(2):
            lanes = slice(part * TILE, (part + 1) * TILE)
            tile = slice(group * width + part * TILE, group * width + (part + 1) * TILE)
            x = x_ref[at, tile].astype(F32)
            dy = jnp.where(live, dy_ref[at, tile].astype(F32), 0.0)
            gain = spread(cols[:8], 96 + 2 * part, low[:8])[:1]
            sides = [
                jnp.broadcast_to(cols[:, 2 * part + k : 2 * part + k + 1], square)
                for k in range(2)
            ]
            step = spread(cols, 32 + 2 * part, low)
            log = jnp.where(low, sides[0], sides[1])
            last = log[TILE - 1 :]
            since = jnp.exp2(log)
            until = jnp.exp2(last - log)
            ahead, back = [], []
            for k in range(2):
                gap = sides[k] - rows[2 * part + k : 2 * part + k + 1]
                ahead.append((jnp.exp2(jnp.minimum(gap, 0.0)) * scores[block]).astype(BF16))
                back.append((jnp.exp2(jnp.minimum(-gap, 0.0)) * scores_t[block]).astype(BF16))
            stepped = x * step
            y = dot(jnp.concatenate(ahead, 1), split(stepped)) + gain * x
            y = y + since * carried[:, lanes]
            y_ref[at, lanes] = jnp.where(live, y, 0.0)
            dx = dot(jnp.concatenate(back, 1), split(dy))
            inner_dx[at, lanes] = step * dx + gain * dy
            out_scale[at, lanes] = step * until
            wdy[at, lanes] = (dy * since).astype(BF16)
            update.append((stepped * until).astype(BF16))
            end.append(jnp.exp2(last))
        end = jnp.concatenate(end, 1)
        ends[block] = jnp.broadcast_to(end, ends.shape[1:])
        state[...] = end * held + dot(b_turned[:, at], jnp.concatenate(update, 1))

    out_y = pltpu.make_async_copy(y_ref, y_hbm.at[group], left.at[0])
    out_y.start()
    state[...] = jnp.zeros_like(state)

    for block in reversed(range(blocks)):
        at = slice(block * TILE, (block + 1) * TILE)
        held = state[...]
        dx = inner_dx[at, :] + out_scale[at, :] * dot(b_ref[at, :], held.astype(BF16))
        dx_ref[at, :] = dx.astype(BF16)
        state[...] = ends[block][:1] * held + dot(c_turned[:, at], wdy[at, :])

    out_dx = pltpu.make_async_copy(dx_ref, dx_hbm.at[:, ours], left.at[1])
    out_dx.start()
    out_y.wait()
    out_dx.wait()


def mix(group, pos, x, dy, b, c, cols, rows, prepared, before):
    tokens, total = x.shape
    state = b.shape[1]
    width = total // RING
    blocks = tokens // TILE
    operands = [pos, x, dy, b, c, cols, rows, *prepared]
    specs = [SMEM] + [VMEM] * (len(operands) - 1)
    alias = {}
    if before is not None:
        alias = {len(operands): 0, len(operands) + 1: 1}
        specs += [HBM, HBM]
        operands += list(before)
    return pl.pallas_call(
        functools.partial(mix_kernel, group),
        out_shape=(
            jax.ShapeDtypeStruct((RING, tokens, width), F32),
            jax.ShapeDtypeStruct((tokens, total), BF16),
        ),
        in_specs=specs,
        out_specs=(HBM, HBM),
        scratch_shapes=[
            pltpu.VMEM((tokens, width), F32),
            pltpu.VMEM((tokens, width), BF16),
            pltpu.VMEM((tokens, width), F32),
            pltpu.VMEM((tokens, width), F32),
            pltpu.VMEM((tokens, width), BF16),
            pltpu.VMEM((state, width), F32),
            pltpu.VMEM((blocks, 8, width), F32),
            pltpu.SemaphoreType.DMA((2,)),
        ],
        input_output_aliases=alias,
        compiler_params=params(),
        cost_estimate=pl.CostEstimate(
            flops=8 * tokens * width * state, bytes_accessed=4 << 20, transcendentals=0
        ),
        name="mix",
    )(*operands)


def finish_kernel(
    pos, c_ref, entries_ref, y_hbm, p0, p1, p7, p3, p5, up_ref, down_ref, out_hbm,
    state, y_all, out_all, arrived, left,
):
    tokens, width = out_all.shape[1:]

    def store(place):
        start = pl.multiple_of(lax.rem(place + along(pos), RING) * width, width)
        target = out_hbm.at[:, pl.ds(start, width)]
        return pltpu.make_async_copy(out_all.at[place], target, left.at[place])

    def load(place):
        source = y_hbm.at[lax.rem(place + along(pos), RING)]
        return pltpu.make_async_copy(source, y_all.at[place], arrived.at[place])

    for place in range(RING):
        load(place).start()

    tiles = [(ref.at[:STATE], ref.at[STATE:PAIR]) for ref in (p0, p1, down_ref, p3)]
    tiles.append((up_ref.at[PAIR:], down_ref.at[PAIR:]))
    tiles += [(ref.at[:STATE], ref.at[STATE:PAIR]) for ref in (p5, up_ref, p7)]
    for place, (first, second) in enumerate(tiles):
        state[place, :, :TILE] = first[...].astype(BF16)
        state[place, :, TILE:] = second[...].astype(BF16)

    def group_of_heads(ahead, carry):
        group = lax.rem(ahead + along(pos), RING)
        scale = scale_of(group, entries_ref, width)
        carried = scale * dot(c_ref[...], state[ahead])
        load(ahead).wait()
        y = y_all[ahead] + carried
        out_all[ahead] = y.astype(BF16)
        store(ahead).start()
        return carry

    lax.fori_loop(0, RING, group_of_heads, 0)
    for place in range(RING):
        store(place).wait()


def finish(pos, c, entries, y, pairs):
    _, tokens, width = y.shape
    return pl.pallas_call(
        finish_kernel,
        in_specs=[SMEM, VMEM, VMEM, HBM] + [VMEM] * len(pairs),
        out_specs=HBM,
        scratch_shapes=[
            pltpu.VMEM((RING, 2 * TILE, width), BF16),
            pltpu.VMEM((RING, tokens, width), F32),
            pltpu.VMEM((RING, tokens, width), BF16),
            pltpu.SemaphoreType.DMA((RING,)),
            pltpu.SemaphoreType.DMA((RING,)),
        ],
        out_shape=jax.ShapeDtypeStruct((tokens, RING * width), BF16),
        compiler_params=params(58),
        cost_estimate=pl.CostEstimate(
            flops=2 * tokens * width * RING * 256, bytes_accessed=10 << 20, transcendentals=0
        ),
        name="finish",
    )(pos, c, entries, y, *pairs)


def back_kernel(
    pos, b_ref, got_ref, p0, p1, p7, p3, p5, up_ref, down_ref, own_ref, send_ref
):
    mine = b_ref[...]
    other = jnp.concatenate([got_ref[RING], got_ref[RING + 1]], 1).astype(BF16)
    opposite = jnp.concatenate([up_ref[FULL:], down_ref[FULL:]], 0)
    for place, ref in enumerate((p0, p1, down_ref, p3, opposite, p5, up_ref, p7)):
        grad = ref[:STATE].astype(BF16)
        own_ref[place] = dot(mine, grad)
        send_ref[place, :TILE] = dot(other, grad)
        send_ref[place, TILE:] = ref[STATE:FULL]


def back(pos, *operands):
    shapes = ((RING, TILE, TILE), (RING, TILE + 8, TILE))
    return small(back_kernel, "back", shapes, pos, *operands, nbytes=4 << 20)


def prompt_dx_kernel(
    pos, own_ref, sent_ref, got_ref, cols_ref, fade_ref, out_hbm, skip_ref, out_all, left
):
    even = is_even(pos)
    low = iota((TILE, TILE), 1) < HALF
    scale = cols_ref[...] * pltpu.roll(fade_ref[...], TILE - 32, 1)[:1]
    width = out_all.shape[2]

    def store(place):
        start = pl.multiple_of(lax.rem(place + along(pos), RING) * width, width)
        target = out_hbm.at[:, pl.ds(start, width)]
        return pltpu.make_async_copy(out_all.at[place], target, left.at[place])

    def group_of_heads(ahead, carry):
        group = lax.rem(ahead + along(pos), RING)
        cols = pltpu.roll(scale, lax.rem(TILE - 4 * group, TILE), 1)
        own, got = own_ref[ahead], got_ref[ahead, :TILE]
        tiles = (jnp.where(even, own, got), jnp.where(even, got, own))
        for part in range(2):
            lanes = slice(part * TILE, (part + 1) * TILE)
            out_all[ahead, :, lanes] = (tiles[part] * spread(cols, 2 * part, low)).astype(BF16)
        store(ahead).start()
        own, got = sent_ref[ahead, TILE : TILE + 8], got_ref[ahead, TILE : TILE + 8]
        skip_ref[group, 0] = jnp.where(even, own, got)
        skip_ref[group, 1] = jnp.where(even, got, own)
        return carry

    lax.fori_loop(0, RING, group_of_heads, 0)
    for place in range(RING):
        store(place).wait()


def prompt_gradient(pos, own, sent, got, cols, fade):
    return pl.pallas_call(
        prompt_dx_kernel,
        in_specs=[SMEM] + [VMEM] * 5,
        out_specs=(HBM, VMEM),
        scratch_shapes=[
            pltpu.VMEM((RING, TILE, 2 * TILE), BF16),
            pltpu.SemaphoreType.DMA((RING,)),
        ],
        out_shape=(
            jax.ShapeDtypeStruct((TILE, RING * 2 * TILE), BF16),
            jax.ShapeDtypeStruct((RING, 2, 8, TILE), F32),
        ),
        compiler_params=params(),
        cost_estimate=pl.CostEstimate(flops=10**6, bytes_accessed=2 << 20, transcendentals=0),
        name="prompt_gradient",
    )(pos, own, sent, got, cols, fade)


def along_z(value, distance):
    pairs = [
        (2 * z + y, 2 * ((z + distance) % RING) + y) for z in range(RING) for y in range(2)
    ]
    return lax.ppermute(value, "sample", pairs)


def swap(value, bit=1):
    return lax.ppermute(value, "sample", [(s, s ^ bit) for s in range(2 * RING)])


def along_dp(value, distance):
    return lax.ppermute(value, "dp", [(i, (i + distance) % 4) for i in range(4)])


def together(*values):
    return lax.optimization_barrier(values)


def body(
    prompt_x, prompt_b, prompt_step, resp_x, resp_b, resp_c, resp_step,
    decay_rate, skip_gain, lengths, prompt_map, resp_cotangent,
):
    place = lax.axis_index("sample")
    pos = lengths[0]
    rate, gain = decay_rate[None], skip_gain[None]
    x, dy, b, c = resp_x[0, 0], resp_cotangent[0, 0], resp_b[0, 0], resp_c[0, 0]

    mine = sum_logs(prompt_step[0], rate)
    other = swap(mine)
    gain, _ = together(gain, mine)
    sent, own, coef, down, up, cols, rows, turned, entries = begin(
        pos, prompt_step[0], rate, gain, prompt_b[0], prompt_x[0], resp_step[0, 0], c, dy
    )
    other, sent = together(other, sent)
    got = swap(sent)
    down, up = along_z(down, -1), along_z(up, 1)

    after_own = jnp.where(place & 1 == 0, other, 0.0)
    after_got = jnp.where(place & 1 == 0, 0.0, mine)

    def add_later(after_own, after_got, total, other, bit):
        later = jnp.where(place & bit == 0, other, 0.0)
        return after_own + later, after_got + later, total + other

    total = mine + other
    other = swap(total, 2)
    entries, _ = together(entries, total)
    rest, gains, kept = other_grads(pos, dy, x, turned, entries)
    after_own, after_got, total = add_later(after_own, after_got, total, other, 2)
    rest, total = together(rest, total)
    other = swap(total, 4)

    b_ready, _ = together(b, rest)
    prepared = prepare(b_ready, c)
    groups = iter(range(RING))

    def within(before, after, count=2):
        for _ in range(count):
            ready, _ = together(x, after)
            before = mix(next(groups), pos, ready, dy, b, c, cols, rows, prepared, before)
        return before

    five, three = pass_first(pos, rest, down, up)
    after_own, after_got, total = add_later(after_own, after_got, total, other, 4)
    gains, five, three, total = together(gains, five, three, total)
    other = swap(total, 8)
    came = swap(gains)
    five, three = along_z(five, -2), along_z(three, 2)
    after_own, after_got, total = add_later(after_own, after_got, total, other, 8)

    down_a, up_a, rest_a, fade = contributions(
        pos, own, got, prompt_b[0], after_own, after_got, kept, came
    )
    down_a, up_a = along_z(down_a, -1), along_z(up_a, 1)
    mixed = within(None, rest_a, 1)
    rest, rest_a, mixed = together(rest, rest_a, mixed)

    seven, one = pass_second(pos, rest, down, up, five, three)
    five, three = pass_first(pos, rest_a, down_a, up_a)
    seven, one, five, three = together(seven, one, five, three)
    seven, one = along_z(seven, -1), along_z(one, 1)
    five, three = along_z(five, -2), along_z(three, 2)
    mixed = within(mixed, fade, 1)
    rest, rest_a, mixed = together(rest, rest_a, mixed)

    grad_own, grad_send = own_tile(pos, rest, seven, one)
    seven, one = pass_second(pos, rest_a, down_a, up_a, five, three)
    grad_send, seven, one = together(grad_send, seven, one)
    grad_got = swap(grad_send)
    seven, one = along_z(seven, -1), along_z(one, 1)
    mixed = within(mixed, grad_own, 1)
    rest_a, mixed = together(rest_a, mixed)
    share = make_share(pos, rest_a, seven, one, grad_own, grad_got)

    others = [along_dp(share, d) for d in (1, 2, 3)]
    mixed = within(mixed, share)
    share, mixed = together(share, mixed)
    message, start = choose(prompt_map, share, *others)

    start_got = swap(start)
    one, seven = along_z(message, -1), along_z(message, 1)
    one, seven, start_got = together(one, seven, start_got)
    pair = make_pair(pos, start, start_got)
    three, five = along_z(one, -2), along_z(seven, 2)
    pair_one, pair_seven = along_z(pair, -1), along_z(pair, 1)
    mixed = within(mixed, pair)
    three, five, pair_one, pair_seven, mixed = together(
        three, five, pair_one, pair_seven, mixed
    )
    up, down = last_step(pos, one, seven, three, five)
    up, down = along_z(up, 1), along_z(down, -1)
    pair_three, pair_five = along_z(pair_one, -2), along_z(pair_seven, 2)
    mixed = within(mixed, pair_one, 1)
    up, down, pair_three, pair_five, mixed = together(up, down, pair_three, pair_five, mixed)
    own_dx, sent = back(pos, prompt_b[0], got, message, one, seven, three, five, up, down)
    got_last = swap(sent)
    pair_one, _ = together(pair_one, sent)
    pair_up, pair_down = last_step(pos, pair_one, pair_seven, pair_three, pair_five)
    pair_up, pair_down = along_z(pair_up, 1), along_z(pair_down, -1)
    prompt_dx, skip = prompt_gradient(pos, own_dx, sent, got_last, coef, fade)
    skip_grad = jnp.sum(skip[:, :, 0].reshape(-1, HALF), 1)
    pair_up, pair_down, skip_grad = together(pair_up, pair_down, skip_grad)
    pairs = [pair, pair_one, pair_seven, pair_three, pair_five, pair_up, pair_down]
    resp_y = finish(pos, c, entries, mixed[0], pairs)
    return (resp_y[None, None], mixed[1][None, None], prompt_dx[None], skip_grad)


def solution(mesh):
    placed = (
        P("dp", "sample", "tensor"),
        P("dp", "sample", None),
        P("dp", "tensor", "sample"),
        P("dp", "sample", None, "tensor"),
        P("dp", "sample", None, None),
        P("dp", "sample", None, None),
        P("dp", "sample", "tensor", None),
        P("tensor"),
        P("tensor"),
        P("dp", "sample"),
        P(),
        P("dp", "sample", None, "tensor"),
    )
    return jax.shard_map(
        body,
        mesh=mesh,
        in_specs=placed,
        out_specs=(
            P("dp", "sample", None, "tensor"),
            P("dp", "sample", None, "tensor"),
            P("dp", "sample", "tensor"),
            P("tensor"),
        ),
        check_vma=False,
    )
```

```python
import functools

import jax
import jax.numpy as jnp
from jax import lax
from jax.experimental import pallas as pl
from jax.experimental.pallas import tpu as pltpu
from jax.sharding import PartitionSpec as P

F32 = jnp.float32
BF16 = jnp.bfloat16
LOG2E = 1.4426950408889634
EXACT = lax.Precision.HIGHEST
TILE = 128
HALF = 64
RING = 8
STATE = 2 * TILE
PAIR = 2 * STATE
FULL = STATE + 8
KEPT = (0, 1, 3, 5, 7)
VMEM = pl.BlockSpec(memory_space=pltpu.VMEM)
SMEM = pl.BlockSpec(memory_space=pltpu.SMEM)
HBM = pl.BlockSpec(memory_space=pltpu.HBM)


def dot(left, right, dims=((1,), (0,)), precision=None):
    return lax.dot_general(
        left, right, (dims, ((), ())), precision=precision, preferred_element_type=F32
    )


def iota(shape, axis):
    return lax.broadcasted_iota(jnp.int32, shape, axis)


def along(pos):
    return lax.axis_index("sample") >> 1


def is_even(pos):
    return lax.axis_index("sample") & 1 == 0


def column(row):
    heads = row.shape[1]
    square = (heads, heads)
    return jnp.sum(jnp.where(iota(square, 0) == iota(square, 1), row, 0.0), 1, keepdims=True)


def params(megabytes=14):
    return pltpu.CompilerParams(vmem_limit_bytes=megabytes << 20)


def spread(cols, first, low):
    return jnp.where(low, cols[:, first : first + 1], cols[:, first + 1 : first + 2])


def sum_logs_kernel(step_ref, rate_ref, out_ref):
    log = -(step_ref[...] * column(rate_ref[...]))
    heads = log.shape[0]
    total = dot(jnp.ones((8, TILE), F32), log, ((1,), (1,)), EXACT)
    blank = jnp.zeros((8, TILE - 2 * heads), F32)
    out_ref[...] = jnp.concatenate([jnp.zeros((8, heads), F32), total, blank], 1)


def sum_logs(step, rate):
    return pl.pallas_call(
        sum_logs_kernel,
        out_shape=jax.ShapeDtypeStruct((8, TILE), F32),
        in_specs=[VMEM, VMEM],
        out_specs=VMEM,
        compiler_params=params(61),
        cost_estimate=pl.CostEstimate(flops=10**5, bytes_accessed=1 << 15, transcendentals=0),
        name="sum_logs",
    )(step, rate)


def scale_of(group, entries_ref, width):
    head = 4 * group + iota((TILE, width), 1) // HALF
    row = iota((TILE, width), 0)
    chosen = (row < 64) & (row % 32 == head)
    return dot(entries_ref[...], chosen.astype(F32).astype(BF16))


def weigh_group(group, dy, entries_ref, weighted):
    scale = scale_of(group, entries_ref, weighted.shape[1])
    weighted[...] = (dy.astype(F32) * scale).astype(BF16)


FIRST = (6, 2, 4)


def begin_kernel(
    pos, *refs
):
    sources, rest = refs[:8], refs[8:]
    (sent_ref, own_ref, coef_ref, down_ref, up_ref, cols_ref, rows_ref, turned,
     entries_ref) = rest[:9]
    targets, (dy_ref, weighted, arrived) = rest[9:16], rest[16:]
    even = is_even(pos)
    length = pos[0]
    tokens, width = weighted.shape
    groups = [lax.rem(place + along(pos), RING) for place in FIRST]
    copies = [
        pltpu.make_async_copy(source, target, arrived.at[index])
        for index, (source, target) in enumerate(zip(sources, targets))
    ]
    for index, group in enumerate(groups):
        at = pl.ds(pl.multiple_of(group * width, width), width)
        copies.append(
            pltpu.make_async_copy(sources[7].at[:, at], dy_ref.at[index], arrived.at[7 + index])
        )
    for copy in copies:
        copy.start()
    for copy in copies[:5]:
        copy.wait()
    ps_ref, rate_ref, gain_ref, pb_ref, px_ref, step_ref, c_ref = targets

    square = (TILE, TILE)
    rate = column(rate_ref[...])
    step = ps_ref[...]
    heads = step.shape[0]
    log = -(step * rate)
    later = (iota(square, 0) > iota(square, 1)).astype(F32)
    coef = jnp.exp(dot(log, later, precision=EXACT)) * step
    cols = jnp.concatenate([coef, jnp.zeros((TILE - heads, TILE), F32)], 0).T
    coef_ref[...] = cols
    low = iota(square, 1) < HALF
    for place in range(RING):
        pair = []
        for part in range(2):
            tile = 2 * place + part
            x = px_ref[:, tile * TILE : (tile + 1) * TILE].astype(F32)
            pair.append(x * spread(cols, 2 * tile, low))
        own_ref[place] = jnp.where(even, pair[0], pair[1]).astype(BF16)
        sent_ref[place] = jnp.where(even, pair[1], pair[0]).astype(BF16).astype(F32)
    sent_ref[RING] = pb_ref[:, :TILE].astype(F32)
    sent_ref[RING + 1] = pb_ref[:, TILE:].astype(F32)

    copies[5].wait()
    copies[6].wait()
    step = step_ref[...]
    log = step * rate * (-LOG2E)
    gain = jnp.broadcast_to(column(gain_ref[...]), (heads, TILE))
    upto = (iota(square, 0) <= iota(square, 1)).astype(F32)
    run = jnp.zeros((heads, 1), F32)
    blank = jnp.zeros((TILE - 2 * heads, TILE), F32)
    for block in range(tokens // TILE):
        at = slice(block * TILE, (block + 1) * TILE)
        turned[:, at] = c_ref[at, :].astype(F32).T.astype(BF16)
        cum = dot(log[:, at], upto, precision=EXACT)
        rows_ref[:, at] = cum
        whole = cum + run
        run = whole[:, TILE - 1 :]
        live = iota((heads, TILE), 1) + block * TILE < length
        entry = jnp.where(live, jnp.exp2(whole), 0.0)
        cols_ref[at, :] = jnp.concatenate([cum, step[:, at], entry, gain], 0).T
        high = entry.astype(BF16).astype(F32)
        entries_ref[at, :] = jnp.concatenate([high, entry - high, blank], 0).T.astype(BF16)

    for index, group in enumerate(groups):
        copies[7 + index].wait()
        weigh_group(group, dy_ref[index], entries_ref, weighted)
        grad = dot(turned[...], weighted[...])
        if FIRST[index] == 4:
            down_ref[PAIR:] = grad[:, :TILE]
            up_ref[PAIR:] = grad[:, TILE:]
        else:
            ref = down_ref if FIRST[index] == 6 else up_ref
            ref[:STATE] = grad[:, :TILE]
            ref[STATE:PAIR] = grad[:, TILE:]


def begin(pos, ps, rate, gain, pb, px, step, c, dy):
    tokens, width = dy.shape
    state = c.shape[1]
    heads = step.shape[0]
    shape = jax.ShapeDtypeStruct
    small_ones = (ps, rate, gain, pb, px, step, c)
    return pl.pallas_call(
        begin_kernel,
        in_specs=[SMEM] + [HBM] * 8,
        out_specs=(VMEM,) * 9,
        scratch_shapes=[pltpu.VMEM(operand.shape, operand.dtype) for operand in small_ones]
        + [
            pltpu.VMEM((len(FIRST), tokens, width // RING), BF16),
            pltpu.VMEM((tokens, width // RING), BF16),
            pltpu.SemaphoreType.DMA((7 + len(FIRST),)),
        ],
        out_shape=(
            shape((RING + 2, TILE, TILE), F32), shape((RING, TILE, TILE), BF16),
            shape((TILE, TILE), F32),
            shape((PAIR + STATE, TILE), F32), shape((PAIR + STATE, TILE), F32),
            shape((tokens, TILE), F32), shape((heads, tokens), F32),
            shape((state, tokens), BF16), shape((tokens, TILE), BF16),
        ),
        compiler_params=params(60),
        cost_estimate=pl.CostEstimate(
            flops=tokens * width * state, bytes_accessed=4 << 20, transcendentals=0
        ),
        name="begin",
    )(pos, *small_ones, dy)


def other_grads_kernel(
    pos, dy_ref, x_ref, turned, entries_ref, rest_ref, send_ref, keep_ref, weighted
):
    even = is_even(pos)
    length = pos[0]
    tokens, width = weighted.shape

    def piece(slot, carry):
        ahead = jnp.where(slot < 1, 0, 2 * slot - 1)
        group = lax.rem(ahead + along(pos), RING)
        at = pl.ds(pl.multiple_of(group * width, width), width)
        weigh_group(group, dy_ref[:, at], entries_ref, weighted)
        grad = dot(turned[...], weighted[...])
        rest_ref[slot, :STATE] = grad[:, :TILE]
        rest_ref[slot, STATE:] = grad[:, TILE:]
        return carry

    def gain_of_group(ahead, carry):
        group = lax.rem(ahead + along(pos), RING)
        gains = [jnp.zeros((1, TILE), F32)] * 2
        for block in range(tokens // TILE):
            at = slice(block * TILE, (block + 1) * TILE)
            live = iota((TILE, TILE), 0) + block * TILE < length
            for part in range(2):
                tile = pl.ds(pl.multiple_of((2 * group + part) * TILE, TILE), TILE)
                product = dy_ref[at, tile].astype(F32) * x_ref[at, tile].astype(F32)
                product = jnp.where(live, product, 0.0)
                gains[part] = gains[part] + jnp.sum(product, 0, keepdims=True)
        gains = [jnp.broadcast_to(gain, (8, TILE)) for gain in gains]
        keep_ref[ahead] = jnp.where(even, gains[0], gains[1])
        send_ref[ahead] = jnp.where(even, gains[1], gains[0])
        return carry

    lax.fori_loop(0, len(KEPT), piece, 0)
    lax.fori_loop(0, RING, gain_of_group, 0)


def other_grads(pos, dy, x, turned, entries):
    tokens, width = dy.shape
    shapes = ((len(KEPT), PAIR, TILE), (RING, 8, TILE), (RING, 8, TILE))
    return pl.pallas_call(
        other_grads_kernel,
        in_specs=[SMEM] + [VMEM] * 4,
        out_specs=(VMEM,) * len(shapes),
        scratch_shapes=[pltpu.VMEM((tokens, width // RING), BF16)],
        out_shape=tuple(jax.ShapeDtypeStruct(shape, F32) for shape in shapes),
        compiler_params=params(),
        cost_estimate=pl.CostEstimate(
            flops=2 * tokens * width * 256, bytes_accessed=8 << 20, transcendentals=0
        ),
        name="other_grads",
    )(pos, dy, x, turned, entries)


def small(kernel, name, shapes, pos, *operands, nbytes=2 << 20):
    return pl.pallas_call(
        kernel,
        out_shape=tuple(jax.ShapeDtypeStruct(shape, F32) for shape in shapes),
        in_specs=[SMEM] + [VMEM] * len(operands),
        out_specs=(VMEM,) * len(shapes),
        compiler_params=params(),
        cost_estimate=pl.CostEstimate(flops=10**6, bytes_accessed=nbytes, transcendentals=0),
        name=name,
    )(pos, *operands)


def half(rows):
    return rows // 16 * 8 + rows % 16


def pass_first_kernel(pos, rest_ref, down_ref, up_ref, five_ref, three_ref):
    rows = five_ref.shape[0]
    cut = half(rows)
    five_ref[:cut] = rest_ref[3, :cut] + down_ref[rows:]
    five_ref[cut:] = rest_ref[3, cut:]
    three_ref[:cut] = rest_ref[2, :cut]
    three_ref[cut:] = rest_ref[2, cut:] + up_ref[rows:]


def pass_first(pos, rest, down, up):
    return small(pass_first_kernel, "pass_first", (rest.shape[1:],) * 2, pos, rest, down, up)


def pass_second_kernel(
    pos, rest_ref, down_ref, up_ref, far_down_ref, far_up_ref, seven_ref, one_ref
):
    rows = seven_ref.shape[0]
    seven_ref[...] = rest_ref[4] + down_ref[:rows] + far_down_ref[...]
    one_ref[...] = rest_ref[1] + up_ref[:rows] + far_up_ref[...]


def pass_second(pos, rest, *operands):
    shapes = (rest.shape[1:],) * 2
    return small(pass_second_kernel, "pass_second", shapes, pos, rest, *operands)


def own_tile_kernel(pos, rest_ref, down_ref, up_ref, own_ref, send_ref):
    even = is_even(pos)
    first, second = slice(0, STATE), slice(STATE, PAIR)
    first = rest_ref[0, first] + down_ref[first] + up_ref[first]
    second = rest_ref[0, second] + down_ref[second] + up_ref[second]
    own_ref[...] = jnp.where(even, first, second)
    send_ref[...] = jnp.where(even, second, first)


def own_tile(pos, *operands):
    return small(own_tile_kernel, "own_tile", ((STATE, TILE),) * 2, pos, *operands)


def contrib_kernel(
    pos, own_ref, got_ref, b_ref, after_ref, after_got_ref, keep_ref, came_ref,
    down_ref, up_ref, rest_ref, fade_ref,
):
    turned = b_ref[...].astype(F32).T.astype(BF16)
    turned_got = jnp.concatenate([got_ref[RING].T, got_ref[RING + 1].T], 0).astype(BF16)
    low = iota((8, TILE), 1) < HALF
    fades = (jnp.exp(after_ref[...]), jnp.exp(after_got_ref[...]))
    fade_ref[...] = fades[0]
    cut = half(FULL)
    for ahead in range(RING):
        place = lax.rem(along(pos) + ahead, RING)
        shift = lax.rem(2 * TILE - 32 - 4 * place - 2 * (lax.axis_index("sample") & 1), TILE)
        scales = [spread(pltpu.roll(fade, shift, 1), 0, low)[:1] for fade in fades]
        own = dot(turned, own_ref[place])
        got = dot(turned_got, got_ref[place].astype(BF16))
        piece = jnp.concatenate(
            [own * scales[0] + got * scales[1], keep_ref[ahead] + came_ref[ahead]], 0
        )
        if ahead == 4:
            down_ref[FULL:] = piece[:cut]
            up_ref[FULL:] = piece[cut:]
        elif ahead in KEPT:
            rest_ref[KEPT.index(ahead)] = piece
        else:
            ref = down_ref if ahead == 6 else up_ref
            ref[:FULL] = piece


def contributions(pos, *operands):
    cut = half(FULL)
    shapes = (
        (FULL + cut, TILE), (2 * FULL - cut, TILE), (len(KEPT), FULL, TILE), (8, TILE),
    )
    return small(contrib_kernel, "contributions", shapes, pos, *operands, nbytes=6 << 20)


def share_kernel(pos, rest_ref, down_ref, up_ref, own_ref, got_ref, share_ref):
    share_ref[:FULL] = rest_ref[0] + down_ref[...] + up_ref[...]
    share_ref[FULL:] = own_ref[...] + got_ref[...]


def make_share(pos, *operands):
    return small(share_kernel, "make_share", ((FULL + STATE, TILE),), pos, *operands)[0]


def choose_kernel(pos, first, second, third, fourth, message_ref, start_ref):
    here = lax.axis_index("dp")
    distance_to_start = (here - pos[here]) & 3
    shares = (first, second, third, fourth)
    start = first[:STATE]
    grad = jnp.zeros((STATE, TILE), F32)
    gains = jnp.zeros((8, TILE), F32)
    for distance, ref in enumerate(shares):
        start = jnp.where(distance_to_start == distance, ref[:STATE], start)
        mine = pos[(here - distance) & 3] == here
        grad = grad + jnp.where(mine, ref[FULL:], 0.0)
        gains = gains + ref[STATE:FULL]
    message_ref[:STATE] = grad
    message_ref[STATE:] = gains
    start_ref[...] = start


def choose(pos, *operands):
    shapes = ((FULL, TILE), (STATE, TILE))
    return small(choose_kernel, "choose", shapes, pos, *operands)


def pair_kernel(pos, own_ref, got_ref, pair_ref):
    even = is_even(pos)
    pair_ref[:STATE] = jnp.where(even, own_ref[...], got_ref[...])
    pair_ref[STATE:] = jnp.where(even, got_ref[...], own_ref[...])


def make_pair(pos, own, got):
    return small(pair_kernel, "make_pair", ((PAIR, TILE),), pos, own, got)[0]


def last_step_kernel(pos, one_ref, seven_ref, three_ref, five_ref, up_ref, down_ref):
    rows = one_ref.shape[0]
    cut = half(rows)
    up_ref[:rows] = seven_ref[...]
    up_ref[rows:] = five_ref[:cut]
    down_ref[:rows] = one_ref[...]
    down_ref[rows:] = three_ref[cut:]


def last_step(pos, one, seven, three, five):
    rows = one.shape[0]
    cut = half(rows)
    shapes = ((rows + cut, TILE), (2 * rows - cut, TILE))
    return small(last_step_kernel, "last_step", shapes, pos, one, seven, three, five)


def prepare_kernel(b_ref, c_ref, scores, scores_t, b_turned, c_turned):
    square = (TILE, TILE)
    upper = iota(square, 0) <= iota(square, 1)
    lower = iota(square, 0) >= iota(square, 1)
    for block in range(scores.shape[0]):
        at = slice(block * TILE, (block + 1) * TILE)
        b_rows, c_rows = b_ref[at, :], c_ref[at, :]
        scores[block] = jnp.where(lower, dot(c_rows, b_rows, ((1,), (1,))), 0.0)
        scores_t[block] = jnp.where(upper, dot(b_rows, c_rows, ((1,), (1,))), 0.0)
        b_turned[:, at] = b_rows.astype(F32).T.astype(BF16)
        c_turned[:, at] = c_rows.astype(F32).T.astype(BF16)


def prepare(b, c):
    tokens, state = b.shape
    square = jax.ShapeDtypeStruct((tokens // TILE, TILE, TILE), F32)
    turned = jax.ShapeDtypeStruct((state, tokens), BF16)
    return pl.pallas_call(
        prepare_kernel,
        out_shape=(square, square, turned, turned),
        in_specs=[VMEM, VMEM],
        out_specs=(VMEM,) * 4,
        compiler_params=params(),
        cost_estimate=pl.CostEstimate(flops=10**8, bytes_accessed=2 << 20, transcendentals=0),
        name="prepare",
    )(b, c)


def mix_kernel(
    group, pos, x_ref, dy_ref, b_ref, c_ref, cols_ref, rows_ref,
    scores, scores_t, b_turned, c_turned, *rest
):
    (
        y_hbm, dx_hbm, y_ref, dx_ref, inner_dx, out_scale, wdy, state, ends, left,
    ) = rest[-10:]
    length = pos[0]
    tokens, width = y_ref.shape
    blocks = tokens // TILE
    square = (TILE, TILE)
    ours = pl.ds(group * width, width)

    low = iota(square, 1) < HALF

    def split(value):
        return jnp.concatenate(
            [jnp.where(low, value, 0.0), jnp.where(low, 0.0, value)], 0
        ).astype(BF16)

    state[...] = jnp.zeros_like(state)

    for block in range(blocks):
        at = slice(block * TILE, (block + 1) * TILE)
        cols = pltpu.roll(cols_ref[at, :], (TILE - 4 * group) % TILE, 1)
        live = iota(square, 0) + block * TILE < length
        rows = rows_ref[group // 2 * 8 : group // 2 * 8 + 8, at]
        rows = rows[4 * (group % 2) : 4 * (group % 2) + 4]
        held = state[...]
        carried = dot(c_ref[at, :], held.astype(BF16))
        update, end = [], []
        for part in range(2):
            lanes = slice(part * TILE, (part + 1) * TILE)
            tile = slice(group * width + part * TILE, group * width + (part + 1) * TILE)
            x = x_ref[at, tile].astype(F32)
            dy = jnp.where(live, dy_ref[at, tile].astype(F32), 0.0)
            gain = spread(cols[:8], 96 + 2 * part, low[:8])[:1]
            sides = [
                jnp.broadcast_to(cols[:, 2 * part + k : 2 * part + k + 1], square)
                for k in range(2)
            ]
            step = spread(cols, 32 + 2 * part, low)
            log = jnp.where(low, sides[0], sides[1])
            last = log[TILE - 1 :]
            since = jnp.exp2(log)
            until = jnp.exp2(last - log)
            ahead, back = [], []
            for k in range(2):
                gap = sides[k] - rows[2 * part + k : 2 * part + k + 1]
                ahead.append((jnp.exp2(jnp.minimum(gap, 0.0)) * scores[block]).astype(BF16))
                back.append((jnp.exp2(jnp.minimum(-gap, 0.0)) * scores_t[block]).astype(BF16))
            stepped = x * step
            y = dot(jnp.concatenate(ahead, 1), split(stepped)) + gain * x
            y = y + since * carried[:, lanes]
            y_ref[at, lanes] = jnp.where(live, y, 0.0).astype(BF16)
            dx = dot(jnp.concatenate(back, 1), split(dy))
            inner_dx[at, lanes] = step * dx + gain * dy
            out_scale[at, lanes] = step * until
            wdy[at, lanes] = (dy * since).astype(BF16)
            update.append((stepped * until).astype(BF16))
            end.append(jnp.exp2(last))
        end = jnp.concatenate(end, 1)
        ends[block] = jnp.broadcast_to(end, ends.shape[1:])
        state[...] = end * held + dot(b_turned[:, at], jnp.concatenate(update, 1))

    out_y = pltpu.make_async_copy(y_ref, y_hbm.at[group], left.at[0])
    out_y.start()
    state[...] = jnp.zeros_like(state)

    for block in reversed(range(blocks)):
        at = slice(block * TILE, (block + 1) * TILE)
        held = state[...]
        dx = inner_dx[at, :] + out_scale[at, :] * dot(b_ref[at, :], held.astype(BF16))
        dx_ref[at, :] = dx.astype(BF16)
        state[...] = ends[block][:1] * held + dot(c_turned[:, at], wdy[at, :])

    out_dx = pltpu.make_async_copy(dx_ref, dx_hbm.at[:, ours], left.at[1])
    out_dx.start()
    out_y.wait()
    out_dx.wait()


def mix(group, pos, x, dy, b, c, cols, rows, prepared, before):
    tokens, total = x.shape
    state = b.shape[1]
    width = total // RING
    blocks = tokens // TILE
    operands = [pos, x, dy, b, c, cols, rows, *prepared]
    specs = [SMEM] + [VMEM] * (len(operands) - 1)
    alias = {}
    if before is not None:
        alias = {len(operands): 0, len(operands) + 1: 1}
        specs += [HBM, HBM]
        operands += list(before)
    return pl.pallas_call(
        functools.partial(mix_kernel, group),
        out_shape=(
            jax.ShapeDtypeStruct((RING, tokens, width), BF16),
            jax.ShapeDtypeStruct((tokens, total), BF16),
        ),
        in_specs=specs,
        out_specs=(HBM, HBM),
        scratch_shapes=[
            pltpu.VMEM((tokens, width), BF16),
            pltpu.VMEM((tokens, width), BF16),
            pltpu.VMEM((tokens, width), F32),
            pltpu.VMEM((tokens, width), F32),
            pltpu.VMEM((tokens, width), BF16),
            pltpu.VMEM((state, width), F32),
            pltpu.VMEM((blocks, 8, width), F32),
            pltpu.SemaphoreType.DMA((2,)),
        ],
        input_output_aliases=alias,
        compiler_params=params(),
        cost_estimate=pl.CostEstimate(
            flops=8 * tokens * width * state, bytes_accessed=4 << 20, transcendentals=0
        ),
        name="mix",
    )(*operands)


def finish_kernel(
    pos, c_ref, entries_ref, y_hbm, p0, p1, p7, p3, p5, up_ref, down_ref, out_hbm,
    state, y_all, out_all, arrived, left,
):
    tokens, width = out_all.shape[1:]

    def store(place):
        start = pl.multiple_of(lax.rem(place + along(pos), RING) * width, width)
        target = out_hbm.at[:, pl.ds(start, width)]
        return pltpu.make_async_copy(out_all.at[place], target, left.at[place])

    def load(place):
        source = y_hbm.at[lax.rem(place + along(pos), RING)]
        return pltpu.make_async_copy(source, y_all.at[place], arrived.at[place])

    for place in range(RING):
        load(place).start()

    tiles = [(ref.at[:STATE], ref.at[STATE:PAIR]) for ref in (p0, p1, down_ref, p3)]
    tiles.append((up_ref.at[PAIR:], down_ref.at[PAIR:]))
    tiles += [(ref.at[:STATE], ref.at[STATE:PAIR]) for ref in (p5, up_ref, p7)]
    for place, (first, second) in enumerate(tiles):
        state[place, :, :TILE] = first[...].astype(BF16)
        state[place, :, TILE:] = second[...].astype(BF16)

    def group_of_heads(ahead, carry):
        group = lax.rem(ahead + along(pos), RING)
        scale = scale_of(group, entries_ref, width)
        carried = scale * dot(c_ref[...], state[ahead])
        load(ahead).wait()
        y = y_all[ahead].astype(F32) + carried
        out_all[ahead] = y.astype(BF16)
        store(ahead).start()
        return carry

    lax.fori_loop(0, RING, group_of_heads, 0)
    for place in range(RING):
        store(place).wait()


def finish(pos, c, entries, y, pairs):
    _, tokens, width = y.shape
    return pl.pallas_call(
        finish_kernel,
        in_specs=[SMEM, VMEM, VMEM, HBM] + [VMEM] * len(pairs),
        out_specs=HBM,
        scratch_shapes=[
            pltpu.VMEM((RING, 2 * TILE, width), BF16),
            pltpu.VMEM((RING, tokens, width), BF16),
            pltpu.VMEM((RING, tokens, width), BF16),
            pltpu.SemaphoreType.DMA((RING,)),
            pltpu.SemaphoreType.DMA((RING,)),
        ],
        out_shape=jax.ShapeDtypeStruct((tokens, RING * width), BF16),
        compiler_params=params(58),
        cost_estimate=pl.CostEstimate(
            flops=2 * tokens * width * RING * 256, bytes_accessed=10 << 20, transcendentals=0
        ),
        name="finish",
    )(pos, c, entries, y, *pairs)


def back_kernel(
    pos, b_ref, got_ref, p0, p1, p7, p3, p5, up_ref, down_ref, own_ref, send_ref
):
    mine = b_ref[...]
    other = jnp.concatenate([got_ref[RING], got_ref[RING + 1]], 1).astype(BF16)
    opposite = jnp.concatenate([up_ref[FULL:], down_ref[FULL:]], 0)
    for place, ref in enumerate((p0, p1, down_ref, p3, opposite, p5, up_ref, p7)):
        grad = ref[:STATE].astype(BF16)
        own_ref[place] = dot(mine, grad)
        send_ref[place, :TILE] = dot(other, grad)
        send_ref[place, TILE:] = ref[STATE:FULL]


def back(pos, *operands):
    shapes = ((RING, TILE, TILE), (RING, TILE + 8, TILE))
    return small(back_kernel, "back", shapes, pos, *operands, nbytes=4 << 20)


def prompt_dx_kernel(
    pos, own_ref, sent_ref, got_ref, cols_ref, fade_ref, out_hbm, skip_ref, out_all, left
):
    even = is_even(pos)
    low = iota((TILE, TILE), 1) < HALF
    scale = cols_ref[...] * pltpu.roll(fade_ref[...], TILE - 32, 1)[:1]
    width = out_all.shape[2]

    def store(place):
        start = pl.multiple_of(lax.rem(place + along(pos), RING) * width, width)
        target = out_hbm.at[:, pl.ds(start, width)]
        return pltpu.make_async_copy(out_all.at[place], target, left.at[place])

    def group_of_heads(ahead, carry):
        group = lax.rem(ahead + along(pos), RING)
        cols = pltpu.roll(scale, lax.rem(TILE - 4 * group, TILE), 1)
        own, got = own_ref[ahead], got_ref[ahead, :TILE]
        tiles = (jnp.where(even, own, got), jnp.where(even, got, own))
        for part in range(2):
            lanes = slice(part * TILE, (part + 1) * TILE)
            out_all[ahead, :, lanes] = (tiles[part] * spread(cols, 2 * part, low)).astype(BF16)
        store(ahead).start()
        own, got = sent_ref[ahead, TILE : TILE + 8], got_ref[ahead, TILE : TILE + 8]
        skip_ref[group, 0] = jnp.where(even, own, got)
        skip_ref[group, 1] = jnp.where(even, got, own)
        return carry

    lax.fori_loop(0, RING, group_of_heads, 0)
    for place in range(RING):
        store(place).wait()


def prompt_gradient(pos, own, sent, got, cols, fade):
    return pl.pallas_call(
        prompt_dx_kernel,
        in_specs=[SMEM] + [VMEM] * 5,
        out_specs=(HBM, VMEM),
        scratch_shapes=[
            pltpu.VMEM((RING, TILE, 2 * TILE), BF16),
            pltpu.SemaphoreType.DMA((RING,)),
        ],
        out_shape=(
            jax.ShapeDtypeStruct((TILE, RING * 2 * TILE), BF16),
            jax.ShapeDtypeStruct((RING, 2, 8, TILE), F32),
        ),
        compiler_params=params(),
        cost_estimate=pl.CostEstimate(flops=10**6, bytes_accessed=2 << 20, transcendentals=0),
        name="prompt_gradient",
    )(pos, own, sent, got, cols, fade)


def along_z(value, distance):
    pairs = [
        (2 * z + y, 2 * ((z + distance) % RING) + y) for z in range(RING) for y in range(2)
    ]
    return lax.ppermute(value, "sample", pairs)


def swap(value, bit=1):
    return lax.ppermute(value, "sample", [(s, s ^ bit) for s in range(2 * RING)])


def along_dp(value, distance):
    return lax.ppermute(value, "dp", [(i, (i + distance) % 4) for i in range(4)])


def together(*values):
    return lax.optimization_barrier(values)


def body(
    prompt_x, prompt_b, prompt_step, resp_x, resp_b, resp_c, resp_step,
    decay_rate, skip_gain, lengths, prompt_map, resp_cotangent,
):
    place = lax.axis_index("sample")
    pos = lengths[0]
    rate, gain = decay_rate[None], skip_gain[None]
    x, dy, b, c = resp_x[0, 0], resp_cotangent[0, 0], resp_b[0, 0], resp_c[0, 0]

    mine = sum_logs(prompt_step[0], rate)
    other = swap(mine)
    gain, _ = together(gain, mine)
    sent, own, coef, down, up, cols, rows, turned, entries = begin(
        pos, prompt_step[0], rate, gain, prompt_b[0], prompt_x[0], resp_step[0, 0], c, dy
    )
    other, sent = together(other, sent)
    got = swap(sent)
    down, up = along_z(down, -1), along_z(up, 1)

    after_own = jnp.where(place & 1 == 0, other, 0.0)
    after_got = jnp.where(place & 1 == 0, 0.0, mine)

    def add_later(after_own, after_got, total, other, bit):
        later = jnp.where(place & bit == 0, other, 0.0)
        return after_own + later, after_got + later, total + other

    total = mine + other
    other = swap(total, 2)
    entries, _ = together(entries, total)
    rest, gains, kept = other_grads(pos, dy, x, turned, entries)
    after_own, after_got, total = add_later(after_own, after_got, total, other, 2)
    rest, total = together(rest, total)
    other = swap(total, 4)

    b_ready, _ = together(b, rest)
    prepared = prepare(b_ready, c)
    groups = iter(range(RING))

    def within(before, after, count=2):
        for _ in range(count):
            ready, _ = together(x, after)
            before = mix(next(groups), pos, ready, dy, b, c, cols, rows, prepared, before)
        return before

    five, three = pass_first(pos, rest, down, up)
    after_own, after_got, total = add_later(after_own, after_got, total, other, 4)
    gains, five, three, total = together(gains, five, three, total)
    other = swap(total, 8)
    came = swap(gains)
    five, three = along_z(five, -2), along_z(three, 2)
    after_own, after_got, total = add_later(after_own, after_got, total, other, 8)

    down_a, up_a, rest_a, fade = contributions(
        pos, own, got, prompt_b[0], after_own, after_got, kept, came
    )
    down_a, up_a = along_z(down_a, -1), along_z(up_a, 1)
    mixed = within(None, rest_a, 1)
    rest, rest_a, mixed = together(rest, rest_a, mixed)

    seven, one = pass_second(pos, rest, down, up, five, three)
    five, three = pass_first(pos, rest_a, down_a, up_a)
    seven, one, five, three = together(seven, one, five, three)
    seven, one = along_z(seven, -1), along_z(one, 1)
    five, three = along_z(five, -2), along_z(three, 2)
    mixed = within(mixed, fade, 1)
    rest, rest_a, mixed = together(rest, rest_a, mixed)

    grad_own, grad_send = own_tile(pos, rest, seven, one)
    seven, one = pass_second(pos, rest_a, down_a, up_a, five, three)
    grad_send, seven, one = together(grad_send, seven, one)
    grad_got = swap(grad_send)
    seven, one = along_z(seven, -1), along_z(one, 1)
    mixed = within(mixed, grad_own, 1)
    rest_a, mixed = together(rest_a, mixed)
    share = make_share(pos, rest_a, seven, one, grad_own, grad_got)

    others = [along_dp(share, d) for d in (1, 2, 3)]
    mixed = within(mixed, share)
    share, mixed = together(share, mixed)
    message, start = choose(prompt_map, share, *others)

    start_got = swap(start)
    one, seven = along_z(message, -1), along_z(message, 1)
    one, seven, start_got = together(one, seven, start_got)
    pair = make_pair(pos, start, start_got)
    three, five = along_z(one, -2), along_z(seven, 2)
    pair_one, pair_seven = along_z(pair, -1), along_z(pair, 1)
    mixed = within(mixed, pair)
    three, five, pair_one, pair_seven, mixed = together(
        three, five, pair_one, pair_seven, mixed
    )
    up, down = last_step(pos, one, seven, three, five)
    up, down = along_z(up, 1), along_z(down, -1)
    pair_three, pair_five = along_z(pair_one, -2), along_z(pair_seven, 2)
    mixed = within(mixed, pair_one, 1)
    up, down, pair_three, pair_five, mixed = together(up, down, pair_three, pair_five, mixed)
    own_dx, sent = back(pos, prompt_b[0], got, message, one, seven, three, five, up, down)
    got_last = swap(sent)
    pair_one, _ = together(pair_one, sent)
    pair_up, pair_down = last_step(pos, pair_one, pair_seven, pair_three, pair_five)
    pair_up, pair_down = along_z(pair_up, 1), along_z(pair_down, -1)
    prompt_dx, skip = prompt_gradient(pos, own_dx, sent, got_last, coef, fade)
    skip_grad = jnp.sum(skip[:, :, 0].reshape(-1, HALF), 1)
    pair_up, pair_down, skip_grad = together(pair_up, pair_down, skip_grad)
    pairs = [pair, pair_one, pair_seven, pair_three, pair_five, pair_up, pair_down]
    resp_y = finish(pos, c, entries, mixed[0], pairs)
    return (resp_y[None, None], mixed[1][None, None], prompt_dx[None], skip_grad)


def solution(mesh):
    placed = (
        P("dp", "sample", "tensor"),
        P("dp", "sample", None),
        P("dp", "tensor", "sample"),
        P("dp", "sample", None, "tensor"),
        P("dp", "sample", None, None),
        P("dp", "sample", None, None),
        P("dp", "sample", "tensor", None),
        P("tensor"),
        P("tensor"),
        P("dp", "sample"),
        P(),
        P("dp", "sample", None, "tensor"),
    )
    return jax.shard_map(
        body,
        mesh=mesh,
        in_specs=placed,
        out_specs=(
            P("dp", "sample", None, "tensor"),
            P("dp", "sample", None, "tensor"),
            P("dp", "sample", "tensor"),
            P("tensor"),
        ),
        check_vma=False,
    )
```
